512 devices in a mesh: dp: 8 (over y, z_hi), ctx: 64 (over z_lo, x, core).
Axes of the slice: x: 4, y: 4, z: 16 (z_hi: 2, z_lo: 8; z = z_hi * 8 + z_lo), core: 2. Of those that a mesh axis runs over, the one named last changes fastest.
Arguments:
- values: bfloat16 [8, 4096, 8192], P('dp', None, 'ctx'), may hold values from -6 to 6
- grads: bfloat16 [8, 4096, 8192], P('dp', None, 'ctx'), may hold values from -6 to 6
- filter_taps: bfloat16 [4096, 8192], P('ctx', 'dp'), may hold values from -6 to 6
Outputs:
- conv_out: bfloat16 [8, 4096, 8192], P('dp', None, 'ctx')
- value_grads: bfloat16 [8, 4096, 8192], P('dp', None, 'ctx')
- filter_grads: float32 [4096, 8192], P('ctx', 'dp')
The draws below stay inside these ranges and needn't reach their ends.
All inputs are finite; a program needn't handle non-finite values.
Results may differ from the reference program's by a relative error of at most 0.022.
Values may be sent and summed in bfloat16 or wider, within the bound.
No kernel may reach another device: no remote copies, remote signals or barrier semaphores. Data moves between devices by JAX's collectives and lax.ppermute only.
A program may use at most 128 MiB of HBM per device.

```python
import math
import jax
import jax.numpy as jnp
from jax import lax

CH = 4096
BATCH = 8
SEQ = 8192
FFT = 16384
FAST = 128
SLOW = 128
N_DP = 8
N_CTX = 64


def block_levels(own_key, shape, split, least, largest):
    def one(axis_at, shards_of):
        steps = jax.random.uniform(jax.random.fold_in(jax.random.fold_in(own_key, 6), axis_at), (shards_of,), jnp.float32, least / len(split), largest / len(split))
        return jnp.repeat(jnp.exp(steps), shape[axis_at] // shards_of).reshape((-1,) + (1,) * (len(shape) - axis_at - 1))

    gain = one(*split[0])
    for cut in split[1:]:
        gain = gain * one(*cut)
    return gain


def bell_draw(own_key, dims, scale, reach, pieces=(), held_as=jnp.bfloat16):
    loudness = block_levels(own_key, dims, pieces, -0.22, 0.18) if pieces else 1.0
    drawn = jax.random.normal(own_key, dims, jnp.float32) * scale * loudness
    return jnp.minimum(jnp.maximum(drawn, -reach), reach).astype(held_as)


def setup_inputs(seed: int = 0) -> dict:
    streams_of = jax.random.split(jax.random.key(seed), 4)
    values = bell_draw(streams_of[0], (BATCH, CH, SEQ), 1.0, 6.0, ((0, 8), (2, 64)))
    grads = bell_draw(streams_of[1], (BATCH, CH, SEQ), 1.0, 6.0, ((0, 8), (2, 64)))
    filter_taps = bell_draw(streams_of[2], (CH, SEQ), 1.0, 6.0, ((0, 64), (1, 8)))
    return dict(values=values, grads=grads, filter_taps=filter_taps)


def build_tables(slow, fast):
    total = slow * fast
    first = jnp.arange(slow // 2, dtype=jnp.int32)
    second = jnp.arange(slow, dtype=jnp.int32)
    inner = jnp.arange(fast, dtype=jnp.int32)
    coarse = (second[:, None] * first[None, :] % slow).astype(jnp.float32) * (2.0 * math.pi / slow)
    twist = (second[:, None] * inner[None, :] % total).astype(jnp.float32) * (2.0 * math.pi / total)
    fine = (inner[:, None] * inner[None, :] % fast).astype(jnp.float32) * (2.0 * math.pi / fast)
    slow_cos = jnp.cos(coarse).astype(jnp.bfloat16)
    slow_sin = jnp.sin(coarse).astype(jnp.bfloat16)
    slow_table = jnp.stack([slow_cos, -slow_sin], axis=0)
    twid_cos = jnp.cos(twist).astype(jnp.bfloat16)
    twid_sin = jnp.sin(twist).astype(jnp.bfloat16)
    fast_cos = jnp.cos(fine).astype(jnp.bfloat16)
    fast_sin = jnp.sin(fine).astype(jnp.bfloat16)
    fwd_real = jnp.stack([fast_cos, fast_sin], axis=0)
    fwd_imag = jnp.stack([-fast_sin, fast_cos], axis=0)
    fwd_table = jnp.stack([fwd_real, fwd_imag], axis=2)
    inv_real = jnp.stack([fast_cos, -fast_sin], axis=0)
    inv_imag = jnp.stack([fast_sin, fast_cos], axis=0)
    inv_table = jnp.stack([inv_real, inv_imag], axis=2)
    return (slow_table, twid_cos, twid_sin, fwd_table, inv_table)

def mix(form, left, right):
    return jnp.einsum(form, left.astype(jnp.float32), right.astype(jnp.float32), precision=lax.Precision.HIGHEST)

def forward_transform(signal, tables):
    slow_table, twid_cos, twid_sin, fwd_table, inv_table = tables
    rows = signal.shape[0]
    blocks = signal.reshape(rows, slow_table.shape[2], twid_cos.shape[1])
    section = mix('pca,hab->hcpb', slow_table, blocks)
    wr, wi = (twid_cos.astype(jnp.float32), twid_sin.astype(jnp.float32))
    part_real, part_imag = (section[:, :, 0], section[:, :, 1])
    twisted = jnp.stack([part_real * wr + part_imag * wi, part_imag * wr - part_real * wi], axis=2).astype(jnp.bfloat16)
    return mix('hcpb,pbqd->hcqd', twisted, fwd_table).astype(jnp.bfloat16)

def inverse_transform(spectrum, tables):
    slow_table, twid_cos, twid_sin, fwd_table, inv_table = tables
    rows = spectrum.shape[0]
    section = mix('hcqd,qdpb->hcpb', spectrum, inv_table)
    wr, wi = (twid_cos.astype(jnp.float32), twid_sin.astype(jnp.float32))
    part_real, part_imag = (section[:, :, 0], section[:, :, 1])
    twisted = jnp.stack([part_real * wr - part_imag * wi, part_imag * wr + part_real * wi], axis=2).astype(jnp.bfloat16)
    result = mix('pca,hcpb->hab', slow_table, twisted)
    return result.reshape(rows, -1)

def spectral_products(u_spec, g_spec, k_spec):
    ur, ui = (u_spec[:, :, 0].astype(jnp.float32), u_spec[:, :, 1].astype(jnp.float32))
    gr, gi = (g_spec[:, :, 0].astype(jnp.float32), g_spec[:, :, 1].astype(jnp.float32))
    kr, ki = (k_spec[:, :, 0].astype(jnp.float32), k_spec[:, :, 1].astype(jnp.float32))
    out_spec = jnp.stack([ur * kr - ui * ki, ur * ki + ui * kr], axis=2).astype(jnp.bfloat16)
    back_spec = jnp.stack([kr * gr + ki * gi, kr * gi - ki * gr], axis=2).astype(jnp.bfloat16)
    taps_spec = jnp.stack([ur * gr + ui * gi, ur * gi - ui * gr], axis=2).astype(jnp.bfloat16)
    return (out_spec, back_spec, taps_spec)

def reference(values, grads, filter_taps):
    tables = build_tables(SLOW, FAST)
    factor = 1.0 / (FFT * math.sqrt(SEQ))
    width = CH // N_CTX

    def one_block(index):
        start = (index * width).astype(jnp.int32)
        taps = lax.dynamic_slice_in_dim(filter_taps, start, width, 0)
        k_spec = forward_transform(taps, tables)
        block_values = lax.dynamic_slice_in_dim(values, start, width, 1)
        block_grads = lax.dynamic_slice_in_dim(grads, start, width, 1)

        def one_sequence(carry, pair):
            u_spec = forward_transform(pair[0], tables)
            g_spec = forward_transform(pair[1], tables)
            out_spec, back_spec, taps_spec = spectral_products(u_spec, g_spec, k_spec)
            conv = (inverse_transform(out_spec, tables) * factor).astype(jnp.bfloat16)
            back = (inverse_transform(back_spec, tables) * factor).astype(jnp.bfloat16)
            carry = carry + inverse_transform(taps_spec, tables)
            return (carry, (conv, back))
        total, (conv, back) = lax.scan(one_sequence, jnp.zeros((width, SEQ), jnp.float32), (block_values, block_grads))
        return (conv, back, total * factor)
    conv, back, taps_grads = lax.map(one_block, jnp.arange(CH // width, dtype=jnp.int32))
    conv_out = jnp.transpose(conv, (1, 0, 2, 3)).reshape(N_DP, CH, SEQ)
    value_grads = jnp.transpose(back, (1, 0, 2, 3)).reshape(N_DP, CH, SEQ)
    return (conv_out, value_grads, taps_grads.reshape(CH, SEQ))
```

```python
import functools
import math

import jax
import jax.numpy as jnp
import numpy as np
from jax import lax
from jax.experimental import pallas as pl
from jax.experimental.pallas import tpu as pltpu
from jax.sharding import Mesh, PartitionSpec as P

SLOW = 128
FAST = 128
TOTAL = SLOW * FAST
HALF = SLOW // 2
ROWS = 80
FACTOR = 1.0 / (TOTAL * math.sqrt(TOTAL // 2))
BLOCK = 8


def tables():
    bf16 = jnp.bfloat16

    def angles(left, right, period):
        steps = (left[:, None] * right[None, :]) % period
        return steps.astype(np.float32) * np.float32(2.0 * math.pi / period)

    rows, first, inner = np.arange(ROWS), np.arange(HALF), np.arange(FAST)
    coarse = angles(rows, first, SLOW)
    twist = angles(rows, inner, TOTAL)
    fine = angles(inner, inner, FAST)
    cast = lambda item: item.astype(bf16)
    slow_cos, slow_sin = cast(np.cos(coarse)), cast(np.sin(coarse))
    twid_cos, twid_sin = cast(np.cos(twist)), cast(np.sin(twist))
    fast_cos, fast_sin = cast(np.cos(fine)), cast(np.sin(fine))
    weight = np.where(rows > HALF, 0.0, np.where(rows % HALF == 0, 1.0, 2.0))
    weight = weight.astype(np.float32)[:, None]
    slow_fwd = np.concatenate([slow_cos, -slow_sin], axis=0)
    slow_inv = np.concatenate(
        [cast(slow_cos.astype(np.float32) * weight), cast(-slow_sin.astype(np.float32) * weight)], axis=0
    ).T
    fast_fwd = np.block([[fast_cos, -fast_sin], [fast_sin, fast_cos]])
    fast_inv = np.block([[fast_cos, fast_sin], [-fast_sin, fast_cos]])
    twid = np.stack([twid_cos, twid_sin]).astype(np.float32)
    return tuple(map(np.ascontiguousarray, (slow_fwd, slow_inv, fast_fwd, fast_inv, twid)))


def dot(left, right):
    return jnp.dot(left, right, preferred_element_type=jnp.float32)


def forward(signal, slow_fwd, twid, fast_fwd):
    lanes = jnp.concatenate([signal[j] for j in range(BLOCK)], axis=1)
    section = dot(slow_fwd[...], lanes)
    wr, wi = twid[0], twid[1]
    parts = []
    for j in range(BLOCK):
        sr = section[:ROWS, j * FAST : (j + 1) * FAST]
        si = section[ROWS:, j * FAST : (j + 1) * FAST]
        parts.append(jnp.concatenate([sr * wr + si * wi, si * wr - sr * wi], axis=1).astype(jnp.bfloat16))
    return dot(jnp.concatenate(parts, axis=0), fast_fwd[...]).astype(jnp.bfloat16)


def inverse(spectrum, out, slow_inv, twid, fast_inv):
    section = dot(spectrum, fast_inv[...])
    wr, wi = twid[0], twid[1]
    parts = []
    for j in range(BLOCK):
        br = section[j * ROWS : (j + 1) * ROWS, :FAST]
        bi = section[j * ROWS : (j + 1) * ROWS, FAST:]
        parts.append(jnp.concatenate([br * wr - bi * wi, bi * wr + br * wi], axis=0).astype(jnp.bfloat16))
    result = dot(slow_inv[...], jnp.concatenate(parts, axis=1)) * FACTOR
    for j in range(BLOCK):
        out[j] = result[:, j * FAST : (j + 1) * FAST].astype(out.dtype)


def halves(spectrum):
    return spectrum[:, :FAST].astype(jnp.float32), spectrum[:, FAST:].astype(jnp.float32)


def joined(real, imag):
    return jnp.concatenate([real, imag], axis=1).astype(jnp.bfloat16)


def conv_kernel(values, taps, slow_fwd, slow_inv, fast_fwd, fast_inv, twid, u_out, k_out, conv):
    u_spec = forward(values, slow_fwd, twid, fast_fwd)
    k_spec = forward(taps, slow_fwd, twid, fast_fwd)
    u_out[...] = u_spec
    k_out[...] = k_spec
    (ur, ui), (kr, ki) = halves(u_spec), halves(k_spec)
    inverse(joined(ur * kr - ui * ki, ur * ki + ui * kr), conv, slow_inv, twid, fast_inv)


def taps_kernel(grads, u_in, slow_fwd, slow_inv, fast_fwd, fast_inv, twid, z_out, taps):
    z_spec = forward(grads, slow_fwd, twid, fast_fwd)
    z_out[...] = z_spec
    (ur, ui), (zr, zi) = halves(u_in[...]), halves(z_spec)
    inverse(joined(ur * zr + ui * zi, ur * zi - ui * zr), taps, slow_inv, twid, fast_inv)


def back_kernel(z_in, k_in, slow_fwd, slow_inv, fast_fwd, fast_inv, twid, back):
    (zr, zi), (kr, ki) = halves(z_in[...]), halves(k_in[...])
    inverse(joined(kr * zr + ki * zi, kr * zi - ki * zr), back, slow_inv, twid, fast_inv)


def call(kernel, signals, outs, consts, flops):
    chans = max(item.shape[0] for item, kind in signals if kind == "x") if any(
        kind == "x" for _, kind in signals
    ) else signals[0][0].shape[0] // ROWS
    specs = {
        "x": pl.BlockSpec((BLOCK, HALF, FAST), lambda i: (i, 0, 0)),
        "s": pl.BlockSpec((BLOCK * ROWS, 2 * FAST), lambda i: (i, 0)),
    }
    shapes = {
        "x": jax.ShapeDtypeStruct((chans, HALF, FAST), jnp.bfloat16),
        "s": jax.ShapeDtypeStruct((chans * ROWS, 2 * FAST), jnp.bfloat16),
    }
    whole = [pl.BlockSpec(item.shape, functools.partial(lambda n, i: (0,) * n, item.ndim)) for item in consts]
    moved = sum(item.size * 2 for item, _ in signals) + sum(shapes[kind].size * 2 for kind in outs)
    return pl.pallas_call(
        kernel,
        grid=(chans // BLOCK,),
        in_specs=[specs[kind] for _, kind in signals] + whole,
        out_specs=[specs[kind] for kind in outs],
        out_shape=[shapes[kind] for kind in outs],
        compiler_params=pltpu.CompilerParams(vmem_limit_bytes=40 * 1024 * 1024),
        cost_estimate=pl.CostEstimate(flops=flops * chans, bytes_accessed=moved, transcendentals=0),
    )(*[item for item, _ in signals], *consts)


def exchange(item, axis):
    return lax.ppermute(item, axis, [(0, 1), (1, 0)])


def local(values, grads, filter_taps):
    ctx = ("zl", "x", "c")
    groups = lax.axis_size(ctx)
    chans = values.shape[1] // groups
    consts = tuple(jnp.asarray(item) for item in tables())
    high = lax.axis_index("zh")
    row = lax.axis_index("y")
    n_row = lax.axis_size("y")
    wide = filter_taps.shape[1]

    def inward(item):
        moved = lax.all_to_all(item.reshape(groups, chans, FAST), ctx, split_axis=0, concat_axis=0, tiled=True)
        return moved.transpose(1, 0, 2)

    def outward(item):
        moved = lax.all_to_all(item.transpose(1, 0, 2), ctx, split_axis=0, concat_axis=0, tiled=True)
        return moved.reshape(1, groups * chans, FAST)

    other = exchange(filter_taps, "zh")
    pair = jnp.stack([jnp.where(high == 0, filter_taps, other), jnp.where(high == 0, other, filter_taps)])
    gathered = lax.all_gather(pair, "y", axis=0, tiled=True)
    taps = gathered.transpose(1, 0, 2).reshape(chans, HALF, FAST)

    v_mine = inward(values)
    g_mine = inward(grads)
    fft = 2 * 2 * ROWS * FAST * (HALF + 2 * FAST)
    u_spec, k_spec, conv = call(conv_kernel, [(v_mine, "x"), (taps, "x")], "ssx", consts, 3 * fft)
    conv_out = outward(conv)
    z_spec, terms = call(taps_kernel, [(g_mine, "x"), (u_spec, "s")], "sx", consts, 2 * fft)
    (back,) = call(back_kernel, [(z_spec, "s"), (k_spec, "s")], "x", consts, fft)
    value_grads = outward(back)

    parts = terms.reshape(chans, n_row, 2, wide).transpose(1, 2, 0, 3)
    total = lax.dynamic_index_in_dim(parts, row, 0, keepdims=False).astype(jnp.float32)
    for step in range(1, n_row):
        block = lax.dynamic_index_in_dim(parts, (row + step) % n_row, 0, keepdims=False)
        arrived = lax.ppermute(block, "y", [(i, (i + step) % n_row) for i in range(n_row)])
        total = total + arrived.astype(jnp.float32)
    mine = jnp.where(high == 0, total[0], total[1])
    sent = jnp.where(high == 0, total[1], total[0]).astype(jnp.bfloat16)
    filter_grads = mine + exchange(sent, "zh").astype(jnp.float32)
    return conv_out, value_grads, filter_grads


def solution(mesh):
    fine = Mesh(mesh.devices.reshape(4, 2, 8, 4, 2), ("y", "zh", "zl", "x", "c"))
    dp, ctx = ("y", "zh"), ("zl", "x", "c")
    tokens = P(dp, None, ctx)
    return jax.shard_map(
        local,
        mesh=fine,
        in_specs=(tokens, tokens, P(ctx, dp)),
        out_specs=(tokens, tokens, P(ctx, dp)),
        check_vma=False,
    )
```

```python
import functools
import math

import jax
import jax.numpy as jnp
import numpy as np
from jax import lax
from jax.experimental import pallas as pl
from jax.experimental.pallas import tpu as pltpu
from jax.sharding import Mesh, PartitionSpec as P

SLOW = 128
FAST = 128
TOTAL = SLOW * FAST
HALF = SLOW // 2
ROWS = 80
FACTOR = 1.0 / (TOTAL * math.sqrt(TOTAL // 2))
NEAR = HALF // 2
RING = 4
QUARTER = HALF // RING
BLOCK = 8


def tables():
    bf16 = jnp.bfloat16

    def angles(left, right, period):
        steps = (left[:, None] * right[None, :]) % period
        return steps.astype(np.float32) * np.float32(2.0 * math.pi / period)

    rows, first, inner = np.arange(ROWS), np.arange(HALF), np.arange(FAST)
    coarse = angles(rows, first, SLOW)
    twist = angles(rows, inner, TOTAL)
    fine = angles(inner, inner, FAST)
    cast = lambda item: item.astype(bf16)
    slow_cos, slow_sin = cast(np.cos(coarse)), cast(np.sin(coarse))
    twid_cos, twid_sin = cast(np.cos(twist)), cast(np.sin(twist))
    fast_cos, fast_sin = cast(np.cos(fine)), cast(np.sin(fine))
    weight = np.where(rows > HALF, 0.0, np.where(rows % HALF == 0, 1.0, 2.0))
    weight = weight.astype(np.float32)[:, None]
    slow_fwd = np.concatenate([slow_cos, -slow_sin], axis=0)
    slow_inv = np.concatenate(
        [cast(slow_cos.astype(np.float32) * weight), cast(-slow_sin.astype(np.float32) * weight)], axis=0
    ).T
    fast_fwd = np.block([[fast_cos, -fast_sin], [fast_sin, fast_cos]])
    fast_inv = np.block([[fast_cos, fast_sin], [-fast_sin, fast_cos]])
    twid = np.stack([twid_cos, twid_sin]).astype(np.float32)
    near = HALF // 2
    slow_half = np.stack([slow_fwd[:, :near], slow_fwd[:, near:]])
    slow_taps = np.stack([np.concatenate(
        [slow_fwd[:, (y - k) % RING * QUARTER : ((y - k) % RING + 1) * QUARTER] for k in range(RING)], axis=1
    ) for y in range(RING)])
    out_half = np.stack([slow_inv[:near], slow_inv[near:]])
    named = dict(slow_half=slow_half, slow_taps=slow_taps, out_half=out_half, out_full=slow_inv,
                 fast_fwd=fast_fwd, fast_inv=fast_inv, twid=twid)
    return {name: np.ascontiguousarray(item) for name, item in named.items()}


def dot(left, right):
    return jnp.dot(left, right, preferred_element_type=jnp.float32)


def lanes(signal):
    return jnp.concatenate([signal[j] for j in range(BLOCK)], axis=1)


def spectrum(section, twid, fast_fwd):
    wr, wi = twid[0], twid[1]
    parts = []
    for j in range(BLOCK):
        sr = section[:ROWS, j * FAST : (j + 1) * FAST]
        si = section[ROWS:, j * FAST : (j + 1) * FAST]
        parts.append(jnp.concatenate([sr * wr + si * wi, si * wr - sr * wi], axis=1).astype(jnp.bfloat16))
    return dot(jnp.concatenate(parts, axis=0), fast_fwd[...])


def inverse(product, out, slow_out, twid, fast_inv):
    section = dot(product, fast_inv[...])
    wr, wi = twid[0], twid[1]
    parts = []
    for j in range(BLOCK):
        br = section[j * ROWS : (j + 1) * ROWS, :FAST]
        bi = section[j * ROWS : (j + 1) * ROWS, FAST:]
        parts.append(jnp.concatenate([br * wr - bi * wi, bi * wr + br * wi], axis=0).astype(jnp.bfloat16))
    result = dot(slow_out, jnp.concatenate(parts, axis=1)) * FACTOR
    for j in range(BLOCK):
        out[j] = result[:, j * FAST : (j + 1) * FAST].astype(out.dtype)


def halves(spec):
    return spec[:, :FAST].astype(jnp.float32), spec[:, FAST:].astype(jnp.float32)


def joined(real, imag):
    return jnp.concatenate([real, imag], axis=1).astype(jnp.bfloat16)


def sign_of(place):
    return jnp.where(place[0] == 0, 1.0, -1.0).astype(jnp.float32)


def first_kernel(place, first, near, fast_fwd, twid, h_out):
    h_out[...] = spectrum(dot(near[0], lanes(first)), twid, fast_fwd).astype(jnp.bfloat16)


def local_kernel(place, h_in, taps, taps_table, slow_out, fast_fwd, fast_inv, twid, k_out, out):
    kr, ki = halves(spectrum(dot(taps_table[0], lanes(taps)), twid, fast_fwd).astype(jnp.bfloat16))
    ki = ki * sign_of(place)
    k_out[...] = joined(kr, ki)
    hr, hi = halves(h_in[...])
    inverse(joined(hr * kr - hi * ki, hr * ki + hi * kr), out, slow_out[0], twid, fast_inv)


def other_kernel(place, second, h_in, near, slow_out, fast_fwd, fast_inv, twid, terms):
    s_spec = spectrum(dot(near[0], lanes(second)), twid, fast_fwd).astype(jnp.bfloat16)
    (hr, hi), (sr, si) = halves(h_in[...]), halves(s_spec)
    inverse(joined(hr * sr + hi * si, (hr * si - hi * sr) * sign_of(place)), terms, slow_out[0], twid, fast_inv)


def full_spectrum(second, crossed, near, far, fast_fwd, twid):
    section = dot(near[0], lanes(second)) + dot(far[0], lanes(crossed))
    return halves(spectrum(section, twid, fast_fwd).astype(jnp.bfloat16))


def own_kernel(
    place, second, crossed, h_in, k_in, near, far, slow_out, out_full, fast_fwd, fast_inv, twid, terms, out
):
    fr, fi = full_spectrum(second, crossed, near, far, fast_fwd, twid)
    hr, hi = halves(h_in[...])
    product = joined(hr * fr + hi * fi, (hr * fi - hi * fr) * sign_of(place))
    inverse(product, terms, out_full[...], twid, fast_inv)
    kr, ki = halves(k_in[...])
    inverse(joined(kr * fr + ki * fi, kr * fi - ki * fr), out, slow_out[0], twid, fast_inv)


def cross_kernel(place, second, crossed, k_in, near, far, slow_out, fast_fwd, fast_inv, twid, out):
    fr, fi = full_spectrum(second, crossed, near, far, fast_fwd, twid)
    kr, ki = halves(k_in[...])
    inverse(joined(kr * fr + ki * fi, kr * fi - ki * fr), out, slow_out[0], twid, fast_inv)


def call(kernel, place, chans, items, outs):
    in_specs, arrays = [], []
    for item, kind, pick in items:
        if kind == "x":
            spec = pl.BlockSpec((BLOCK,) + item.shape[1:], lambda i, p, pick=pick: (pick(p) + i, 0, 0))
        elif kind == "s":
            spec = pl.BlockSpec((BLOCK * ROWS, 2 * FAST), lambda i, p, pick=pick: (pick(p) + i, 0))
        elif kind == "t":
            spec = pl.BlockSpec((1,) + item.shape[1:], lambda i, p, pick=pick: (pick(p), 0, 0))
        else:
            spec = pl.BlockSpec(item.shape, lambda i, p, n=item.ndim: (0,) * n)
        in_specs.append(spec)
        arrays.append(item)
    out_specs, shapes = [], []
    for rows in outs:
        if rows:
            out_specs.append(pl.BlockSpec((BLOCK, rows, FAST), lambda i, p: (i, 0, 0)))
            shapes.append(jax.ShapeDtypeStruct((chans, rows, FAST), jnp.bfloat16))
        else:
            out_specs.append(pl.BlockSpec((BLOCK * ROWS, 2 * FAST), lambda i, p: (i, 0)))
            shapes.append(jax.ShapeDtypeStruct((chans * ROWS, 2 * FAST), jnp.bfloat16))
    return pl.pallas_call(
        kernel,
        grid_spec=pltpu.PrefetchScalarGridSpec(
            num_scalar_prefetch=1, grid=(chans // BLOCK,), in_specs=in_specs, out_specs=out_specs
        ),
        out_shape=shapes,
        compiler_params=pltpu.CompilerParams(vmem_limit_bytes=40 * 1024 * 1024),
        cost_estimate=pl.CostEstimate(flops=1, bytes_accessed=1, transcendentals=0),
    )(place, *arrays)


def swap(item, axis):
    return lax.ppermute(item, axis, [(0, 1), (1, 0)])


def diagonal(item):
    return lax.ppermute(item, ("zh", "zb"), [(0, 3), (1, 2), (2, 1), (3, 0)])


def pick_half(item, index, axis=0):
    size = item.shape[axis] // 2
    return lax.dynamic_slice_in_dim(item, index * size, size, axis)


def ordered(low, near, far, axis=0):
    return jnp.concatenate([jnp.where(low, near, far), jnp.where(low, far, near)], axis=axis)


def local(values, grads, filter_taps):
    span = ("za", "x", "c")
    n_span = lax.axis_size(span)
    chans = values.shape[1] // n_span
    own = chans // 2
    consts = {name: jnp.asarray(item) for name, item in tables().items()}
    zh, zb, y = lax.axis_index("zh"), lax.axis_index("zb"), lax.axis_index("y")
    low, left = zb == 0, zh == 0
    place = jnp.stack([zb, y]).astype(jnp.int32)

    def ring(item, step, reach=RING):
        pairs = [(i, (i + step) % RING) for i in range(RING) if (i + step) % RING < reach]
        return lax.ppermute(item, "y", pairs)

    def spread(item):
        return item.reshape(2, n_span, own, FAST).transpose(1, 0, 2, 3).reshape(n_span, chans, FAST)

    def move(item):
        return lax.all_to_all(item, span, split_axis=0, concat_axis=0, tiled=True)

    taps = filter_taps.reshape(own, HALF // 8, FAST)
    across = diagonal(taps)

    v_parts, g_parts = spread(values), spread(grads)
    first_raw = move(jnp.where(low, v_parts, g_parts))
    second_in = jnp.where(low, g_parts, v_parts)
    swapped = swap(jnp.stack([taps, across]), "zb")
    first_raw, second_in, swapped = lax.optimization_barrier((first_raw, second_in, swapped))

    first = first_raw.transpose(1, 0, 2)
    crossed_own = swap(pick_half(first, 1 - zb), "zb")
    second = move(second_in).transpose(1, 0, 2)
    near_taps = ordered(left, taps, swapped[1], axis=1)
    far_taps = ordered(left, swapped[0], across, axis=1)
    taps = ordered(low, near_taps, far_taps)
    taps = jnp.concatenate([taps] + [ring(taps, step) for step in range(1, RING)], axis=1)

    n_own = own // BLOCK
    at_start, at_own, at_far = (lambda p: 0), (lambda p: p[0] * n_own), (lambda p: (1 - p[0]) * n_own)
    here, there, row = (lambda p: p[0]), (lambda p: 1 - p[0]), (lambda p: p[1])
    near = (consts["slow_half"], "t", here)
    far = (consts["slow_half"], "t", there)
    out_near = (consts["out_half"], "t", here)
    out_start = (consts["out_half"], "t", at_start)
    out_full = (consts["out_full"], None, None)
    fast_fwd, fast_inv, twid = [(consts[name], None, None) for name in ("fast_fwd", "fast_inv", "twid")]

    (h_spec,) = call(first_kernel, place, chans, [(first, "x", at_start), near, fast_fwd, twid], [0])
    k_spec, local_out = call(
        local_kernel, place, chans,
        [(h_spec, "s", at_start), (taps, "x", at_start), (consts["slow_taps"], "t", row), out_near,
         fast_fwd, fast_inv, twid], [0, NEAR],
    )
    local_in = local_out.transpose(1, 0, 2)
    local_in, crossed_own, second, first = lax.optimization_barrier((local_in, crossed_own, second, first))

    local_back = move(local_in)
    mine = pick_half(first, zb)
    crossed_a = swap(mine[: own // 2], "zb")
    mine_b, crossed_a = lax.optimization_barrier((mine[own // 2 :], crossed_a))
    crossed_far = jnp.concatenate([crossed_a, swap(mine_b, "zb")])
    own_terms, out_own = call(
        own_kernel, place, own,
        [(second, "x", at_own), (crossed_own, "x", at_start), (h_spec, "s", at_own), (k_spec, "s", at_own),
         near, far, out_near, out_full, fast_fwd, fast_inv, twid], [HALF, NEAR],
    )
    (far_terms,) = call(
        other_kernel, place, own,
        [(second, "x", at_far), (h_spec, "s", at_far), near, out_start, fast_fwd, fast_inv, twid], [NEAR],
    )

    def along(item, reach):
        total = None
        for step in range(RING):
            index = jnp.minimum((y + step) % RING, reach - 1)
            block = lax.dynamic_slice_in_dim(item, index * QUARTER, QUARTER, 1)
            block = (ring(block, step, reach) if step else block).astype(jnp.float32)
            total = block if total is None else total + block
        return total

    own_sum = along(own_terms, RING)
    far_sum = jnp.where(y < RING // 2, along(far_terms, RING // 2), 0.0)
    crossed_far, local_back, own_sum, far_sum = lax.optimization_barrier(
        (crossed_far, local_back, own_sum, far_sum)
    )

    (out_far,) = call(
        cross_kernel, place, own,
        [(second, "x", at_far), (crossed_far, "x", at_start), (k_spec, "s", at_far), near, far, out_near,
         fast_fwd, fast_inv, twid], [NEAR],
    )
    cross_back = move(ordered(low, out_own, out_far).transpose(1, 0, 2))

    def gathered(item):
        return item.reshape(n_span, 2, own, FAST).transpose(1, 0, 2, 3).reshape(values.shape)

    conv_out = gathered(jnp.where(low, local_back, cross_back))
    value_grads = gathered(jnp.where(low, cross_back, local_back))

    far_here, far_there = pick_half(far_sum, zh, 1), pick_half(far_sum, 1 - zh, 1)
    own_here, own_there = pick_half(own_sum, zh, 1), pick_half(own_sum, 1 - zh, 1)
    arrived = swap(jnp.stack([far_here, own_there]).astype(jnp.bfloat16), "zb").astype(jnp.float32)
    passed = diagonal((far_there + arrived[1]).astype(jnp.bfloat16)).astype(jnp.float32)
    filter_grads = own_here + arrived[0] + passed
    return conv_out, value_grads, filter_grads.reshape(filter_taps.shape)


def solution(mesh):
    fine = Mesh(mesh.devices.reshape(RING, 2, 2, 4, 4, 2), ("y", "zh", "zb", "za", "x", "c"))
    dp, ctx = ("y", "zh"), ("zb", "za", "x", "c")
    tokens = P(dp, None, ctx)
    return jax.shard_map(
        local,
        mesh=fine,
        in_specs=(tokens, tokens, P(ctx, dp)),
        out_specs=(tokens, tokens, P(ctx, dp)),
        check_vma=False,
    )
```

```python
import functools
import math

import jax
import jax.numpy as jnp
import numpy as np
from jax import lax
from jax.experimental import pallas as pl
from jax.experimental.pallas import tpu as pltpu
from jax.sharding import Mesh, PartitionSpec as P

SLOW = 128
FAST = 128
TOTAL = SLOW * FAST
HALF = SLOW // 2
ROWS = 80
FACTOR = 1.0 / (TOTAL * math.sqrt(TOTAL // 2))
NEAR = HALF // 2
RING = 4
QUARTER = HALF // RING
BLOCK = 8


def tables():
    bf16 = jnp.bfloat16

    def angles(left, right, period):
        steps = (left[:, None] * right[None, :]) % period
        return steps.astype(np.float32) * np.float32(2.0 * math.pi / period)

    rows, first, inner = np.arange(ROWS), np.arange(HALF), np.arange(FAST)
    coarse = angles(rows, first, SLOW)
    twist = angles(rows, inner, TOTAL)
    fine = angles(inner, inner, FAST)
    cast = lambda item: item.astype(bf16)
    slow_cos, slow_sin = cast(np.cos(coarse)), cast(np.sin(coarse))
    twid_cos, twid_sin = cast(np.cos(twist)), cast(np.sin(twist))
    fast_cos, fast_sin = cast(np.cos(fine)), cast(np.sin(fine))
    weight = np.where(rows > HALF, 0.0, np.where(rows % HALF == 0, 1.0, 2.0))
    weight = weight.astype(np.float32)[:, None]
    slow_fwd = np.concatenate([slow_cos, -slow_sin], axis=0)
    slow_inv = np.concatenate(
        [cast(slow_cos.astype(np.float32) * weight), cast(-slow_sin.astype(np.float32) * weight)], axis=0
    ).T
    fast_fwd = np.block([[fast_cos, -fast_sin], [fast_sin, fast_cos]])
    fast_inv = np.block([[fast_cos, fast_sin], [-fast_sin, fast_cos]])
    twid = np.stack([twid_cos, twid_sin]).astype(np.float32)
    near = HALF // 2
    slow_half = np.stack([slow_fwd[:, :near], slow_fwd[:, near:]])
    slow_taps = np.stack([np.concatenate(
        [slow_fwd[:, (y - k) % RING * QUARTER : ((y - k) % RING + 1) * QUARTER] for k in range(RING)], axis=1
    ) for y in range(RING)])
    out_half = np.stack([slow_inv[:near], slow_inv[near:]])
    named = dict(slow_half=slow_half, slow_taps=slow_taps, out_half=out_half, out_full=slow_inv,
                 fast_fwd=fast_fwd, fast_inv=fast_inv, twid=twid)
    return {name: np.ascontiguousarray(item) for name, item in named.items()}


def dot(left, right):
    return jnp.dot(left, right, preferred_element_type=jnp.float32)


def lanes(signal):
    return jnp.concatenate([signal[j] for j in range(BLOCK)], axis=1)


def spectrum(section, twid, fast_fwd):
    wr, wi = twid[0], twid[1]
    parts = []
    for j in range(BLOCK):
        sr = section[:ROWS, j * FAST : (j + 1) * FAST]
        si = section[ROWS:, j * FAST : (j + 1) * FAST]
        parts.append(jnp.concatenate([sr * wr + si * wi, si * wr - sr * wi], axis=1).astype(jnp.bfloat16))
    return dot(jnp.concatenate(parts, axis=0), fast_fwd[...])


def inverse(product, out, slow_out, twid, fast_inv):
    section = dot(product, fast_inv[...])
    wr, wi = twid[0], twid[1]
    parts = []
    for j in range(BLOCK):
        br = section[j * ROWS : (j + 1) * ROWS, :FAST]
        bi = section[j * ROWS : (j + 1) * ROWS, FAST:]
        parts.append(jnp.concatenate([br * wr - bi * wi, bi * wr + br * wi], axis=0).astype(jnp.bfloat16))
    result = dot(slow_out, jnp.concatenate(parts, axis=1)) * FACTOR
    for j in range(BLOCK):
        out[j] = result[:, j * FAST : (j + 1) * FAST].astype(out.dtype)


def halves(spec):
    return spec[:, :FAST].astype(jnp.float32), spec[:, FAST:].astype(jnp.float32)


def joined(real, imag):
    return jnp.concatenate([real, imag], axis=1).astype(jnp.bfloat16)


def sign_of(place):
    return jnp.where(place[0] == 0, 1.0, -1.0).astype(jnp.float32)


def first_kernel(place, first, near, fast_fwd, twid, h_out):
    h_out[...] = spectrum(dot(near[0], lanes(first)), twid, fast_fwd).astype(jnp.bfloat16)


def local_kernel(place, h_in, taps, taps_table, slow_out, fast_fwd, fast_inv, twid, k_out, out):
    kr, ki = halves(spectrum(dot(taps_table[0], lanes(taps)), twid, fast_fwd).astype(jnp.bfloat16))
    ki = ki * sign_of(place)
    k_out[...] = joined(kr, ki)
    hr, hi = halves(h_in[...])
    inverse(joined(hr * kr - hi * ki, hr * ki + hi * kr), out, slow_out[0], twid, fast_inv)


def other_kernel(place, second, h_in, near, slow_out, fast_fwd, fast_inv, twid, terms):
    s_spec = spectrum(dot(near[0], lanes(second)), twid, fast_fwd).astype(jnp.bfloat16)
    (hr, hi), (sr, si) = halves(h_in[...]), halves(s_spec)
    inverse(joined(hr * sr + hi * si, (hr * si - hi * sr) * sign_of(place)), terms, slow_out[0], twid, fast_inv)


def full_spectrum(second, crossed, near, far, fast_fwd, twid):
    section = dot(near[0], lanes(second)) + dot(far[0], lanes(crossed))
    return halves(spectrum(section, twid, fast_fwd).astype(jnp.bfloat16))


def own_kernel(
    place, second, crossed, h_in, k_in, near, far, slow_out, out_full, fast_fwd, fast_inv, twid, terms, out
):
    fr, fi = full_spectrum(second, crossed, near, far, fast_fwd, twid)
    hr, hi = halves(h_in[...])
    product = joined(hr * fr + hi * fi, (hr * fi - hi * fr) * sign_of(place))
    inverse(product, terms, out_full[...], twid, fast_inv)
    kr, ki = halves(k_in[...])
    inverse(joined(kr * fr + ki * fi, kr * fi - ki * fr), out, slow_out[0], twid, fast_inv)


def cross_kernel(place, second, crossed, k_in, near, far, slow_out, fast_fwd, fast_inv, twid, out):
    fr, fi = full_spectrum(second, crossed, near, far, fast_fwd, twid)
    kr, ki = halves(k_in[...])
    inverse(joined(kr * fr + ki * fi, kr * fi - ki * fr), out, slow_out[0], twid, fast_inv)


def call(kernel, place, chans, items, outs):
    in_specs, arrays = [], []
    for item, kind, pick in items:
        if kind == "x":
            spec = pl.BlockSpec((BLOCK,) + item.shape[1:], lambda i, p, pick=pick: (pick(p) + i, 0, 0))
        elif kind == "s":
            spec = pl.BlockSpec((BLOCK * ROWS, 2 * FAST), lambda i, p, pick=pick: (pick(p) + i, 0))
        elif kind == "t":
            spec = pl.BlockSpec((1,) + item.shape[1:], lambda i, p, pick=pick: (pick(p), 0, 0))
        else:
            spec = pl.BlockSpec(item.shape, lambda i, p, n=item.ndim: (0,) * n)
        in_specs.append(spec)
        arrays.append(item)
    out_specs, shapes = [], []
    for rows in outs:
        if rows:
            out_specs.append(pl.BlockSpec((BLOCK, rows, FAST), lambda i, p: (i, 0, 0)))
            shapes.append(jax.ShapeDtypeStruct((chans, rows, FAST), jnp.bfloat16))
        else:
            out_specs.append(pl.BlockSpec((BLOCK * ROWS, 2 * FAST), lambda i, p: (i, 0)))
            shapes.append(jax.ShapeDtypeStruct((chans * ROWS, 2 * FAST), jnp.bfloat16))
    return pl.pallas_call(
        kernel,
        grid_spec=pltpu.PrefetchScalarGridSpec(
            num_scalar_prefetch=1, grid=(chans // BLOCK,), in_specs=in_specs, out_specs=out_specs
        ),
        out_shape=shapes,
        compiler_params=pltpu.CompilerParams(vmem_limit_bytes=56 * 1024 * 1024),
        cost_estimate=pl.CostEstimate(flops=1, bytes_accessed=1, transcendentals=0),
    )(place, *arrays)


def swap(item, axis):
    return lax.ppermute(item, axis, [(0, 1), (1, 0)])


def diagonal(item):
    return lax.ppermute(item, ("zh", "zb"), [(0, 3), (1, 2), (2, 1), (3, 0)])


def pick_half(item, index, axis=0):
    size = item.shape[axis] // 2
    return lax.dynamic_slice_in_dim(item, index * size, size, axis)


def ordered(low, near, far, axis=0):
    return jnp.concatenate([jnp.where(low, near, far), jnp.where(low, far, near)], axis=axis)


def local(values, grads, filter_taps):
    span = ("za", "x", "c")
    n_span = lax.axis_size(span)
    chans = values.shape[1] // n_span
    own = chans // 2
    consts = {name: jnp.asarray(item) for name, item in tables().items()}
    zh, zb, y = lax.axis_index("zh"), lax.axis_index("zb"), lax.axis_index("y")
    low, left = zb == 0, zh == 0
    place = jnp.stack([zb, y]).astype(jnp.int32)

    def ring(item, step):
        return lax.ppermute(item, "y", [(i, (i + step) % RING) for i in range(RING)])

    def spread(item):
        return item.reshape(2, n_span, own, FAST).transpose(1, 0, 2, 3).reshape(n_span, chans, FAST)

    def move(item):
        return lax.all_to_all(item, span, split_axis=0, concat_axis=0, tiled=True)

    taps = filter_taps.reshape(own, HALF // 8, FAST)
    across = diagonal(taps)

    v_parts, g_parts = spread(values), spread(grads)
    first_raw = move(jnp.where(low, v_parts, g_parts))
    second_in = jnp.where(low, g_parts, v_parts)
    swapped = swap(jnp.stack([taps, across]), "zb")
    first_raw, second_in, swapped = lax.optimization_barrier((first_raw, second_in, swapped))

    first = first_raw.transpose(1, 0, 2)

    def crossing(item, gate=None):
        if gate is None:
            return swap(item, "zb")
        item, gate = lax.optimization_barrier((item, gate))
        return swap(item, "zb"), gate

    quarter = own // 2
    to_own, to_far = pick_half(first, 1 - zb), pick_half(first, zb)
    cross_1 = crossing(to_own[:quarter])
    cross_2, cross_1 = crossing(to_own[quarter:], cross_1)
    crossed_own = jnp.concatenate([cross_1, cross_2])

    second = move(second_in).transpose(1, 0, 2)
    near_taps = ordered(left, taps, swapped[1], axis=1)
    far_taps = ordered(left, swapped[0], across, axis=1)
    taps = ordered(low, near_taps, far_taps)
    taps = jnp.concatenate([taps] + [ring(taps, step) for step in range(1, RING)], axis=1)

    n_own = own // BLOCK
    at_start, at_own, at_far = (lambda p: 0), (lambda p: p[0] * n_own), (lambda p: (1 - p[0]) * n_own)
    here, there, row = (lambda p: p[0]), (lambda p: 1 - p[0]), (lambda p: p[1])
    near = (consts["slow_half"], "t", here)
    far = (consts["slow_half"], "t", there)
    out_near = (consts["out_half"], "t", here)
    out_start = (consts["out_half"], "t", at_start)
    out_full = (consts["out_full"], None, None)
    fast_fwd, fast_inv, twid = [(consts[name], None, None) for name in ("fast_fwd", "fast_inv", "twid")]

    (h_spec,) = call(first_kernel, place, chans, [(first, "x", at_start), near, fast_fwd, twid], [0])
    k_spec, local_out = call(
        local_kernel, place, chans,
        [(h_spec, "s", at_start), (taps, "x", at_start), (consts["slow_taps"], "t", row), out_near,
         fast_fwd, fast_inv, twid], [0, NEAR],
    )
    local_in, crossed_own = lax.optimization_barrier((local_out.transpose(1, 0, 2), crossed_own))
    local_back = move(local_in)
    cross_3, crossed_own = crossing(to_far[:quarter], crossed_own)
    own_terms, out_own = call(
        own_kernel, place, own,
        [(second, "x", at_own), (crossed_own, "x", at_start), (h_spec, "s", at_own), (k_spec, "s", at_own),
         near, far, out_near, out_full, fast_fwd, fast_inv, twid], [HALF, NEAR],
    )
    cross_4, cross_3 = crossing(to_far[quarter:], cross_3)
    crossed_far = jnp.concatenate([cross_3, cross_4])
    (far_terms,) = call(
        other_kernel, place, own,
        [(second, "x", at_far), (h_spec, "s", at_far), near, out_start, fast_fwd, fast_inv, twid], [NEAR],
    )

    sums = None
    for step in range(RING):
        to = (y + step) % RING
        block = jnp.stack([
            lax.dynamic_slice_in_dim(own_terms, to * QUARTER, QUARTER, 1),
            lax.dynamic_slice_in_dim(far_terms, jnp.minimum(to, 1) * QUARTER, QUARTER, 1),
        ])
        block = (ring(block, step) if step else block).astype(jnp.float32)
        sums = block if sums is None else sums + block
    crossed_far, local_back, sums = lax.optimization_barrier((crossed_far, local_back, sums))

    own_sum, far_sum = sums[0], jnp.where(y < RING // 2, sums[1], 0.0)
    far_here, far_there = pick_half(far_sum, zh, 1), pick_half(far_sum, 1 - zh, 1)
    own_here, own_there = pick_half(own_sum, zh, 1), pick_half(own_sum, 1 - zh, 1)
    arrived = swap(jnp.stack([far_here, own_there]).astype(jnp.bfloat16), "zb").astype(jnp.float32)
    passed = diagonal((far_there + arrived[1]).astype(jnp.bfloat16)).astype(jnp.float32)
    filter_grads = own_here + arrived[0] + passed

    (out_far,) = call(
        cross_kernel, place, own,
        [(second, "x", at_far), (crossed_far, "x", at_start), (k_spec, "s", at_far), near, far, out_near,
         fast_fwd, fast_inv, twid], [NEAR],
    )
    cross_back = move(ordered(low, out_own, out_far).transpose(1, 0, 2))

    def gathered(item):
        return item.reshape(n_span, 2, own, FAST).transpose(1, 0, 2, 3).reshape(values.shape)

    conv_out = gathered(jnp.where(low, local_back, cross_back))
    value_grads = gathered(jnp.where(low, cross_back, local_back))
    return conv_out, value_grads, filter_grads.reshape(filter_taps.shape)


def solution(mesh):
    fine = Mesh(mesh.devices.reshape(RING, 2, 2, 4, 4, 2), ("y", "zh", "zb", "za", "x", "c"))
    dp, ctx = ("y", "zh"), ("zb", "za", "x", "c")
    tokens = P(dp, None, ctx)
    return jax.shard_map(
        local,
        mesh=fine,
        in_specs=(tokens, tokens, P(ctx, dp)),
        out_specs=(tokens, tokens, P(ctx, dp)),
        check_vma=False,
    )
```

```python
import functools
import math

import jax
import jax.numpy as jnp
import numpy as np
from jax import lax
from jax.experimental import pallas as pl
from jax.experimental.pallas import tpu as pltpu
from jax.sharding import Mesh, PartitionSpec as P

SLOW = 128
FAST = 128
TOTAL = SLOW * FAST
HALF = SLOW // 2
ROWS = 80
FACTOR = 1.0 / (TOTAL * math.sqrt(TOTAL // 2))
NEAR = HALF // 2
RING = 4
QUARTER = HALF // RING
BLOCK = 8
LONG = 30 * 10**9


def tables():
    bf16 = jnp.bfloat16

    def angles(left, right, period):
        steps = (left[:, None] * right[None, :]) % period
        return steps.astype(np.float32) * np.float32(2.0 * math.pi / period)

    rows, first, inner = np.arange(ROWS), np.arange(HALF), np.arange(FAST)
    coarse = angles(rows, first, SLOW)
    twist = angles(rows, inner, TOTAL)
    fine = angles(inner, inner, FAST)
    cast = lambda item: item.astype(bf16)
    slow_cos, slow_sin = cast(np.cos(coarse)), cast(np.sin(coarse))
    twid_cos, twid_sin = cast(np.cos(twist)), cast(np.sin(twist))
    fast_cos, fast_sin = cast(np.cos(fine)), cast(np.sin(fine))
    weight = np.where(rows > HALF, 0.0, np.where(rows % HALF == 0, 1.0, 2.0))
    weight = weight.astype(np.float32)[:, None]
    slow_fwd = np.concatenate([slow_cos, -slow_sin], axis=0)
    slow_inv = np.concatenate(
        [cast(slow_cos.astype(np.float32) * weight), cast(-slow_sin.astype(np.float32) * weight)], axis=0
    ).T
    fast_fwd = np.block([[fast_cos, -fast_sin], [fast_sin, fast_cos]])
    fast_inv = np.block([[fast_cos, fast_sin], [-fast_sin, fast_cos]])
    twid = np.stack([twid_cos, twid_sin]).astype(np.float32)
    near = HALF // 2
    slow_half = np.stack([slow_fwd[:, :near], slow_fwd[:, near:]])
    slow_taps = np.stack([np.concatenate(
        [slow_fwd[:, (y - k) % RING * QUARTER : ((y - k) % RING + 1) * QUARTER] for k in range(RING)], axis=1
    ) for y in range(RING)])
    out_half = np.stack([slow_inv[:near], slow_inv[near:]])
    named = dict(slow_half=slow_half, slow_taps=slow_taps, out_half=out_half, out_full=slow_inv,
                 fast_fwd=fast_fwd, fast_inv=fast_inv, twid=twid)
    return {name: np.ascontiguousarray(item) for name, item in named.items()}


def dot(left, right):
    return jnp.dot(left, right, preferred_element_type=jnp.float32)


def lanes(signal):
    return jnp.concatenate([signal[j] for j in range(BLOCK)], axis=1)


def spectrum(section, twid, fast_fwd):
    wr, wi = twid[0], twid[1]
    parts = []
    for j in range(BLOCK):
        sr = section[:ROWS, j * FAST : (j + 1) * FAST]
        si = section[ROWS:, j * FAST : (j + 1) * FAST]
        parts.append(jnp.concatenate([sr * wr + si * wi, si * wr - sr * wi], axis=1).astype(jnp.bfloat16))
    return dot(jnp.concatenate(parts, axis=0), fast_fwd[...])


def inverse(product, out, slow_out, twid, fast_inv):
    section = dot(product, fast_inv[...])
    wr, wi = twid[0], twid[1]
    parts = []
    for j in range(BLOCK):
        br = section[j * ROWS : (j + 1) * ROWS, :FAST]
        bi = section[j * ROWS : (j + 1) * ROWS, FAST:]
        parts.append(jnp.concatenate([br * wr - bi * wi, bi * wr + br * wi], axis=0).astype(jnp.bfloat16))
    result = dot(slow_out, jnp.concatenate(parts, axis=1)) * FACTOR
    for j in range(BLOCK):
        out[j] = result[:, j * FAST : (j + 1) * FAST].astype(out.dtype)


def halves(spec):
    return spec[:, :FAST].astype(jnp.float32), spec[:, FAST:].astype(jnp.float32)


def joined(real, imag):
    return jnp.concatenate([real, imag], axis=1).astype(jnp.bfloat16)


def sign_of(place):
    return jnp.where(place[0] == 0, 1.0, -1.0).astype(jnp.float32)


def first_kernel(place, first, near, fast_fwd, twid, h_out):
    h_out[...] = spectrum(dot(near[0], lanes(first)), twid, fast_fwd).astype(jnp.bfloat16)


def local_kernel(place, h_in, taps, taps_table, slow_out, fast_fwd, fast_inv, twid, k_out, out):
    kr, ki = halves(spectrum(dot(taps_table[0], lanes(taps)), twid, fast_fwd).astype(jnp.bfloat16))
    ki = ki * sign_of(place)
    k_out[...] = joined(kr, ki)
    hr, hi = halves(h_in[...])
    inverse(joined(hr * kr - hi * ki, hr * ki + hi * kr), out, slow_out[0], twid, fast_inv)


def other_kernel(place, second, h_in, near, slow_out, fast_fwd, fast_inv, twid, terms):
    s_spec = spectrum(dot(near[0], lanes(second)), twid, fast_fwd).astype(jnp.bfloat16)
    (hr, hi), (sr, si) = halves(h_in[...]), halves(s_spec)
    inverse(joined(hr * sr + hi * si, (hr * si - hi * sr) * sign_of(place)), terms, slow_out[0], twid, fast_inv)


def full_spectrum(second, crossed, near, far, fast_fwd, twid):
    section = dot(near[0], lanes(second)) + dot(far[0], lanes(crossed))
    return halves(spectrum(section, twid, fast_fwd).astype(jnp.bfloat16))


def own_kernel(
    place, second, crossed, h_in, k_in, near, far, slow_out, out_full, fast_fwd, fast_inv, twid, terms, out
):
    fr, fi = full_spectrum(second, crossed, near, far, fast_fwd, twid)
    hr, hi = halves(h_in[...])
    product = joined(hr * fr + hi * fi, (hr * fi - hi * fr) * sign_of(place))
    inverse(product, terms, out_full[...], twid, fast_inv)
    kr, ki = halves(k_in[...])
    inverse(joined(kr * fr + ki * fi, kr * fi - ki * fr), out, slow_out[0], twid, fast_inv)


def cross_kernel(place, second, crossed, k_in, near, far, slow_out, fast_fwd, fast_inv, twid, out):
    fr, fi = full_spectrum(second, crossed, near, far, fast_fwd, twid)
    kr, ki = halves(k_in[...])
    inverse(joined(kr * fr + ki * fi, kr * fi - ki * fr), out, slow_out[0], twid, fast_inv)


def call(kernel, place, chans, items, outs, flops=1):
    in_specs, arrays = [], []
    for item, kind, pick in items:
        if kind == "x":
            spec = pl.BlockSpec((BLOCK,) + item.shape[1:], lambda i, p, pick=pick: (pick(p) + i, 0, 0))
        elif kind == "s":
            spec = pl.BlockSpec((BLOCK * ROWS, 2 * FAST), lambda i, p, pick=pick: (pick(p) + i, 0))
        elif kind == "t":
            spec = pl.BlockSpec((1,) + item.shape[1:], lambda i, p, pick=pick: (pick(p), 0, 0))
        else:
            spec = pl.BlockSpec(item.shape, lambda i, p, n=item.ndim: (0,) * n)
        in_specs.append(spec)
        arrays.append(item)
    out_specs, shapes = [], []
    for rows in outs:
        if rows:
            out_specs.append(pl.BlockSpec((BLOCK, rows, FAST), lambda i, p: (i, 0, 0)))
            shapes.append(jax.ShapeDtypeStruct((chans, rows, FAST), jnp.bfloat16))
        else:
            out_specs.append(pl.BlockSpec((BLOCK * ROWS, 2 * FAST), lambda i, p: (i, 0)))
            shapes.append(jax.ShapeDtypeStruct((chans * ROWS, 2 * FAST), jnp.bfloat16))
    return pl.pallas_call(
        kernel,
        grid_spec=pltpu.PrefetchScalarGridSpec(
            num_scalar_prefetch=1, grid=(chans // BLOCK,), in_specs=in_specs, out_specs=out_specs
        ),
        out_shape=shapes,
        compiler_params=pltpu.CompilerParams(vmem_limit_bytes=20 * 1024 * 1024),
        cost_estimate=pl.CostEstimate(flops=flops, bytes_accessed=1, transcendentals=0),
    )(place, *arrays)


def swap(item, axis):
    return lax.ppermute(item, axis, [(0, 1), (1, 0)])


def diagonal(item):
    return lax.ppermute(item, ("zh", "zb"), [(0, 3), (1, 2), (2, 1), (3, 0)])


def pick_half(item, index, axis=0):
    size = item.shape[axis] // 2
    return lax.dynamic_slice_in_dim(item, index * size, size, axis)


def ordered(low, near, far, axis=0):
    return jnp.concatenate([jnp.where(low, near, far), jnp.where(low, far, near)], axis=axis)


def local(values, grads, filter_taps):
    span = ("za", "x", "c")
    n_span = lax.axis_size(span)
    chans = values.shape[1] // n_span
    own = chans // 2
    consts = {name: jnp.asarray(item) for name, item in tables().items()}
    zh, zb, y = lax.axis_index("zh"), lax.axis_index("zb"), lax.axis_index("y")
    low, left = zb == 0, zh == 0
    place = jnp.stack([zb, y]).astype(jnp.int32)

    def ring(item, step):
        return lax.ppermute(item, "y", [(i, (i + step) % RING) for i in range(RING)])

    def spread(item):
        return item.reshape(2, n_span, own, FAST).transpose(1, 0, 2, 3).reshape(n_span, chans, FAST)

    def move(item):
        return lax.all_to_all(item, span, split_axis=0, concat_axis=0, tiled=True)

    taps = filter_taps.reshape(own, HALF // 8, FAST)
    far_here, own_there, far_there = swap(taps, "zb"), swap(taps, "zh"), diagonal(taps)

    v_parts, g_parts = spread(values), spread(grads)
    first_raw = move(jnp.where(low, v_parts, g_parts))
    second_in = jnp.where(low, g_parts, v_parts)
    first_raw, second_in, far_here, own_there, far_there = lax.optimization_barrier(
        (first_raw, second_in, far_here, own_there, far_there)
    )

    first = first_raw.transpose(1, 0, 2)
    n_own = own // BLOCK
    at_start, at_own, at_far = (lambda p: 0), (lambda p: p[0] * n_own), (lambda p: (1 - p[0]) * n_own)
    here, there, row = (lambda p: p[0]), (lambda p: 1 - p[0]), (lambda p: p[1])
    near = (consts["slow_half"], "t", here)
    far = (consts["slow_half"], "t", there)
    out_near = (consts["out_half"], "t", here)
    out_start = (consts["out_half"], "t", at_start)
    out_full = (consts["out_full"], None, None)
    fast_fwd, fast_inv, twid = [(consts[name], None, None) for name in ("fast_fwd", "fast_inv", "twid")]

    (h_spec,) = call(first_kernel, place, chans, [(first, "x", at_start), near, fast_fwd, twid], [0])
    quarter = own // 2
    to_own, to_far = pick_half(first, 1 - zb), pick_half(first, zb)
    cross_own, cross_far = swap(to_own, "zb"), swap(to_far, "zb")

    second = move(second_in).transpose(1, 0, 2)
    near_taps = ordered(left, taps, own_there, axis=1)
    far_taps = ordered(left, far_here, far_there, axis=1)
    taps = ordered(low, near_taps, far_taps)
    taps = jnp.concatenate([taps] + [ring(taps, step) for step in range(1, RING)], axis=1)
    (far_terms,) = call(
        other_kernel, place, own,
        [(second, "x", at_far), (h_spec, "s", at_far), near, out_start, fast_fwd, fast_inv, twid], [NEAR],
    )
    taps, cross_own, far_terms = lax.optimization_barrier((taps, cross_own, far_terms))

    k_spec, local_out = call(
        local_kernel, place, chans,
        [(h_spec, "s", at_start), (taps, "x", at_start), (consts["slow_taps"], "t", row), out_near,
         fast_fwd, fast_inv, twid], [0, NEAR],
    )
    local_back = move(local_out.transpose(1, 0, 2))
    own_terms, out_own = call(
        own_kernel, place, own,
        [(second, "x", at_own), (cross_own, "x", at_start), (h_spec, "s", at_own), (k_spec, "s", at_own),
         near, far, out_near, out_full, fast_fwd, fast_inv, twid], [HALF, NEAR],
    )

    sums = None
    for step in range(RING):
        to = (y + step) % RING
        block = jnp.stack([
            lax.dynamic_slice_in_dim(own_terms, to * QUARTER, QUARTER, 1),
            lax.dynamic_slice_in_dim(far_terms, jnp.minimum(to, 1) * QUARTER, QUARTER, 1),
        ])
        block = (ring(block, step) if step else block).astype(jnp.float32)
        sums = block if sums is None else sums + block
    (out_far,) = call(
        cross_kernel, place, own,
        [(second, "x", at_far), (cross_far, "x", at_start), (k_spec, "s", at_far), near, far, out_near,
         fast_fwd, fast_inv, twid], [NEAR], flops=LONG,
    )
    cross_in = ordered(low, out_own, out_far).transpose(1, 0, 2)
    cross_in, local_back, sums = lax.optimization_barrier((cross_in, local_back, sums))
    cross_back = move(cross_in)

    own_sum, far_sum = sums[0], jnp.where(y < RING // 2, sums[1], 0.0)
    far_here, far_there = pick_half(far_sum, zh, 1), pick_half(far_sum, 1 - zh, 1)
    own_here, own_there = pick_half(own_sum, zh, 1), pick_half(own_sum, 1 - zh, 1)
    arrived = swap(jnp.stack([far_here, own_there]).astype(jnp.bfloat16), "zb").astype(jnp.float32)
    passed = diagonal((far_there + arrived[1]).astype(jnp.bfloat16)).astype(jnp.float32)
    filter_grads = own_here + arrived[0] + passed

    def gathered(item):
        return item.reshape(n_span, 2, own, FAST).transpose(1, 0, 2, 3).reshape(values.shape)

    conv_out = gathered(jnp.where(low, local_back, cross_back))
    value_grads = gathered(jnp.where(low, cross_back, local_back))
    return conv_out, value_grads, filter_grads.reshape(filter_taps.shape)


def solution(mesh):
    fine = Mesh(mesh.devices.reshape(RING, 2, 2, 4, 4, 2), ("y", "zh", "zb", "za", "x", "c"))
    dp, ctx = ("y", "zh"), ("zb", "za", "x", "c")
    tokens = P(dp, None, ctx)
    return jax.shard_map(
        local,
        mesh=fine,
        in_specs=(tokens, tokens, P(ctx, dp)),
        out_specs=(tokens, tokens, P(ctx, dp)),
        check_vma=False,
    )
```

```python
import functools
import math

import jax
import jax.numpy as jnp
import numpy as np
from jax import lax
from jax.experimental import pallas as pl
from jax.experimental.pallas import tpu as pltpu
from jax.sharding import Mesh, PartitionSpec as P

SLOW = 128
FAST = 128
TOTAL = SLOW * FAST
HALF = SLOW // 2
ROWS = 80
FACTOR = 1.0 / (TOTAL * math.sqrt(TOTAL // 2))
NEAR = HALF // 2
RING = 4
QUARTER = HALF // RING
BLOCK = 8
LONG = 45 * 10**9


def tables():
    bf16 = jnp.bfloat16

    def angles(left, right, period):
        steps = (left[:, None] * right[None, :]) % period
        return steps.astype(np.float32) * np.float32(2.0 * math.pi / period)

    rows, first, inner = np.arange(ROWS), np.arange(HALF), np.arange(FAST)
    coarse = angles(rows, first, SLOW)
    twist = angles(rows, inner, TOTAL)
    fine = angles(inner, inner, FAST)
    cast = lambda item: item.astype(bf16)
    slow_cos, slow_sin = cast(np.cos(coarse)), cast(np.sin(coarse))
    twid_cos, twid_sin = cast(np.cos(twist)), cast(np.sin(twist))
    fast_cos, fast_sin = cast(np.cos(fine)), cast(np.sin(fine))
    weight = np.where(rows > HALF, 0.0, np.where(rows % HALF == 0, 1.0, 2.0))
    weight = weight.astype(np.float32)[:, None]
    slow_fwd = np.concatenate([slow_cos, -slow_sin], axis=0)
    slow_inv = np.concatenate(
        [cast(slow_cos.astype(np.float32) * weight), cast(-slow_sin.astype(np.float32) * weight)], axis=0
    ).T
    fast_fwd = np.block([[fast_cos, -fast_sin], [fast_sin, fast_cos]])
    fast_inv = np.block([[fast_cos, fast_sin], [-fast_sin, fast_cos]])
    twid = np.stack([twid_cos, twid_sin]).astype(np.float32)
    near = HALF // 2
    slow_half = np.stack([slow_fwd[:, :near], slow_fwd[:, near:]])
    slow_taps = np.stack([np.concatenate(
        [slow_fwd[:, (y - k) % RING * QUARTER : ((y - k) % RING + 1) * QUARTER] for k in range(RING)], axis=1
    ) for y in range(RING)])
    out_half = np.stack([slow_inv[:near], slow_inv[near:]])
    named = dict(slow_half=slow_half, slow_taps=slow_taps, out_half=out_half, out_full=slow_inv,
                 fast_fwd=fast_fwd, fast_inv=fast_inv, twid=twid)
    return {name: np.ascontiguousarray(item) for name, item in named.items()}


def dot(left, right):
    return jnp.dot(left, right, preferred_element_type=jnp.float32)


def lanes(signal):
    return jnp.concatenate([signal[j] for j in range(BLOCK)], axis=1)


def spectrum(section, twid, fast_fwd):
    wr, wi = twid[0], twid[1]
    parts = []
    for j in range(BLOCK):
        sr = section[:ROWS, j * FAST : (j + 1) * FAST]
        si = section[ROWS:, j * FAST : (j + 1) * FAST]
        parts.append(jnp.concatenate([sr * wr + si * wi, si * wr - sr * wi], axis=1).astype(jnp.bfloat16))
    return dot(jnp.concatenate(parts, axis=0), fast_fwd[...])


def inverse(product, out, slow_out, twid, fast_inv):
    section = dot(product, fast_inv[...])
    wr, wi = twid[0], twid[1]
    parts = []
    for j in range(BLOCK):
        br = section[j * ROWS : (j + 1) * ROWS, :FAST]
        bi = section[j * ROWS : (j + 1) * ROWS, FAST:]
        parts.append(jnp.concatenate([br * wr - bi * wi, bi * wr + br * wi], axis=0).astype(jnp.bfloat16))
    result = dot(slow_out, jnp.concatenate(parts, axis=1)) * FACTOR
    for j in range(BLOCK):
        out[j] = result[:, j * FAST : (j + 1) * FAST].astype(out.dtype)


def halves(spec):
    return spec[:, :FAST].astype(jnp.float32), spec[:, FAST:].astype(jnp.float32)


def joined(real, imag):
    return jnp.concatenate([real, imag], axis=1).astype(jnp.bfloat16)


def sign_of(place):
    return jnp.where(place[0] == 0, 1.0, -1.0).astype(jnp.float32)


def first_kernel(place, first, near, fast_fwd, twid, h_out):
    h_out[...] = spectrum(dot(near[0], lanes(first)), twid, fast_fwd).astype(jnp.bfloat16)


def local_kernel(place, h_in, taps, taps_table, slow_out, fast_fwd, fast_inv, twid, k_out, out):
    kr, ki = halves(spectrum(dot(taps_table[0], lanes(taps)), twid, fast_fwd).astype(jnp.bfloat16))
    ki = ki * sign_of(place)
    k_out[...] = joined(kr, ki)
    hr, hi = halves(h_in[...])
    inverse(joined(hr * kr - hi * ki, hr * ki + hi * kr), out, slow_out[0], twid, fast_inv)


def other_kernel(place, second, h_in, near, slow_out, fast_fwd, fast_inv, twid, terms):
    s_spec = spectrum(dot(near[0], lanes(second)), twid, fast_fwd).astype(jnp.bfloat16)
    (hr, hi), (sr, si) = halves(h_in[...]), halves(s_spec)
    inverse(joined(hr * sr + hi * si, (hr * si - hi * sr) * sign_of(place)), terms, slow_out[0], twid, fast_inv)


def full_spectrum(second, crossed, near, far, fast_fwd, twid):
    section = dot(near[0], lanes(second)) + dot(far[0], lanes(crossed))
    return halves(spectrum(section, twid, fast_fwd).astype(jnp.bfloat16))


def own_kernel(
    place, second, crossed, h_in, k_in, near, far, slow_out, out_full, fast_fwd, fast_inv, twid, terms, out
):
    fr, fi = full_spectrum(second, crossed, near, far, fast_fwd, twid)
    hr, hi = halves(h_in[...])
    product = joined(hr * fr + hi * fi, (hr * fi - hi * fr) * sign_of(place))
    inverse(product, terms, out_full[...], twid, fast_inv)
    kr, ki = halves(k_in[...])
    inverse(joined(kr * fr + ki * fi, kr * fi - ki * fr), out, slow_out[0], twid, fast_inv)


def cross_kernel(place, second, crossed, k_in, near, far, slow_out, fast_fwd, fast_inv, twid, out):
    fr, fi = full_spectrum(second, crossed, near, far, fast_fwd, twid)
    kr, ki = halves(k_in[...])
    inverse(joined(kr * fr + ki * fi, kr * fi - ki * fr), out, slow_out[0], twid, fast_inv)


def call(kernel, place, chans, items, outs, flops=1):
    in_specs, arrays = [], []
    for item, kind, pick in items:
        if kind == "x":
            spec = pl.BlockSpec((BLOCK,) + item.shape[1:], lambda i, p, pick=pick: (pick(p) + i, 0, 0))
        elif kind == "s":
            spec = pl.BlockSpec((BLOCK * ROWS, 2 * FAST), lambda i, p, pick=pick: (pick(p) + i, 0))
        elif kind == "t":
            spec = pl.BlockSpec((1,) + item.shape[1:], lambda i, p, pick=pick: (pick(p), 0, 0))
        else:
            spec = pl.BlockSpec(item.shape, lambda i, p, n=item.ndim: (0,) * n)
        in_specs.append(spec)
        arrays.append(item)
    out_specs, shapes = [], []
    for rows in outs:
        if rows:
            out_specs.append(pl.BlockSpec((BLOCK, rows, FAST), lambda i, p: (i, 0, 0)))
            shapes.append(jax.ShapeDtypeStruct((chans, rows, FAST), jnp.bfloat16))
        else:
            out_specs.append(pl.BlockSpec((BLOCK * ROWS, 2 * FAST), lambda i, p: (i, 0)))
            shapes.append(jax.ShapeDtypeStruct((chans * ROWS, 2 * FAST), jnp.bfloat16))
    return pl.pallas_call(
        kernel,
        grid_spec=pltpu.PrefetchScalarGridSpec(
            num_scalar_prefetch=1, grid=(chans // BLOCK,), in_specs=in_specs, out_specs=out_specs
        ),
        out_shape=shapes,
        compiler_params=pltpu.CompilerParams(vmem_limit_bytes=20 * 1024 * 1024),
        cost_estimate=pl.CostEstimate(flops=flops, bytes_accessed=1, transcendentals=0),
    )(place, *arrays)


def swap(item, axis):
    return lax.ppermute(item, axis, [(0, 1), (1, 0)])


def diagonal(item):
    return lax.ppermute(item, ("zh", "zb"), [(0, 3), (1, 2), (2, 1), (3, 0)])


def pick_half(item, index, axis=0):
    size = item.shape[axis] // 2
    return lax.dynamic_slice_in_dim(item, index * size, size, axis)


def ordered(low, near, far, axis=0):
    return jnp.concatenate([jnp.where(low, near, far), jnp.where(low, far, near)], axis=axis)


def local(values, grads, filter_taps):
    span = ("za", "x", "c")
    n_span = lax.axis_size(span)
    chans = values.shape[1] // n_span
    own = chans // 2
    consts = {name: jnp.asarray(item) for name, item in tables().items()}
    zh, zb, y = lax.axis_index("zh"), lax.axis_index("zb"), lax.axis_index("y")
    low, left = zb == 0, zh == 0
    place = jnp.stack([zb, y]).astype(jnp.int32)

    def ring(item, step):
        return lax.ppermute(item, "y", [(i, (i + step) % RING) for i in range(RING)])

    def spread(item):
        return item.reshape(2, n_span, own, FAST).transpose(1, 0, 2, 3).reshape(n_span, chans, FAST)

    def move(item):
        return lax.all_to_all(item, span, split_axis=0, concat_axis=0, tiled=True)

    taps = filter_taps.reshape(own, HALF // 8, FAST)
    far_here, far_there = swap(taps, "zb"), diagonal(taps)

    v_parts, g_parts = spread(values), spread(grads)
    first_raw = move(jnp.where(low, v_parts, g_parts))
    second_in = jnp.where(low, g_parts, v_parts)
    first_raw, second_in, far_here, far_there = lax.optimization_barrier(
        (first_raw, second_in, far_here, far_there)
    )
    own_there = swap(far_there, "zb")

    first = first_raw.transpose(1, 0, 2)
    n_own = own // BLOCK
    at_start, at_own, at_far = (lambda p: 0), (lambda p: p[0] * n_own), (lambda p: (1 - p[0]) * n_own)
    here, there, row = (lambda p: p[0]), (lambda p: 1 - p[0]), (lambda p: p[1])
    near = (consts["slow_half"], "t", here)
    far = (consts["slow_half"], "t", there)
    out_near = (consts["out_half"], "t", here)
    out_start = (consts["out_half"], "t", at_start)
    out_full = (consts["out_full"], None, None)
    fast_fwd, fast_inv, twid = [(consts[name], None, None) for name in ("fast_fwd", "fast_inv", "twid")]

    (h_spec,) = call(first_kernel, place, chans, [(first, "x", at_start), near, fast_fwd, twid], [0])
    quarter = own // 2
    to_own, to_far = pick_half(first, 1 - zb), pick_half(first, zb)
    cross_own = swap(to_own, "zb")
    cross_own, to_far = lax.optimization_barrier((cross_own, to_far))
    cross_far = swap(to_far, "zb")

    second = move(second_in).transpose(1, 0, 2)
    near_taps = ordered(left, taps, own_there, axis=1)
    far_taps = ordered(left, far_here, far_there, axis=1)
    taps = ordered(low, near_taps, far_taps)
    taps = jnp.concatenate([taps] + [ring(taps, step) for step in range(1, RING)], axis=1)
    (far_terms,) = call(
        other_kernel, place, own,
        [(second, "x", at_far), (h_spec, "s", at_far), near, out_start, fast_fwd, fast_inv, twid], [NEAR],
    )

    k_spec, local_out = call(
        local_kernel, place, chans,
        [(h_spec, "s", at_start), (taps, "x", at_start), (consts["slow_taps"], "t", row), out_near,
         fast_fwd, fast_inv, twid], [0, NEAR],
    )
    local_back = move(local_out.transpose(1, 0, 2))
    own_terms, out_own = call(
        own_kernel, place, own,
        [(second, "x", at_own), (cross_own, "x", at_start), (h_spec, "s", at_own), (k_spec, "s", at_own),
         near, far, out_near, out_full, fast_fwd, fast_inv, twid], [HALF, NEAR],
    )

    sums = None
    for step in range(RING):
        to = (y + step) % RING
        block = jnp.stack([
            lax.dynamic_slice_in_dim(own_terms, to * QUARTER, QUARTER, 1),
            lax.dynamic_slice_in_dim(far_terms, jnp.minimum(to, 1) * QUARTER, QUARTER, 1),
        ])
        block = (ring(block, step) if step else block).astype(jnp.float32)
        sums = block if sums is None else sums + block
    (out_far,) = call(
        cross_kernel, place, own,
        [(second, "x", at_far), (cross_far, "x", at_start), (k_spec, "s", at_far), near, far, out_near,
         fast_fwd, fast_inv, twid], [NEAR], flops=LONG,
    )
    cross_in = ordered(low, out_own, out_far).transpose(1, 0, 2)
    cross_in, local_back, sums = lax.optimization_barrier((cross_in, local_back, sums))
    cross_back = move(cross_in)

    own_sum, far_sum = sums[0], jnp.where(y < RING // 2, sums[1], 0.0)
    far_here, far_there = pick_half(far_sum, zh, 1), pick_half(far_sum, 1 - zh, 1)
    own_here, own_there = pick_half(own_sum, zh, 1), pick_half(own_sum, 1 - zh, 1)
    arrived = swap(jnp.stack([far_here, own_there]).astype(jnp.bfloat16), "zb").astype(jnp.float32)
    passed = diagonal((far_there + arrived[1]).astype(jnp.bfloat16)).astype(jnp.float32)
    filter_grads = own_here + arrived[0] + passed

    def gathered(item):
        return item.reshape(n_span, 2, own, FAST).transpose(1, 0, 2, 3).reshape(values.shape)

    conv_out = gathered(jnp.where(low, local_back, cross_back))
    value_grads = gathered(jnp.where(low, cross_back, local_back))
    return conv_out, value_grads, filter_grads.reshape(filter_taps.shape)


def solution(mesh):
    fine = Mesh(mesh.devices.reshape(RING, 2, 2, 4, 4, 2), ("y", "zh", "zb", "za", "x", "c"))
    dp, ctx = ("y", "zh"), ("zb", "za", "x", "c")
    tokens = P(dp, None, ctx)
    return jax.shard_map(
        local,
        mesh=fine,
        in_specs=(tokens, tokens, P(ctx, dp)),
        out_specs=(tokens, tokens, P(ctx, dp)),
        check_vma=False,
    )
```

```python
import functools
import math

import jax
import jax.numpy as jnp
import numpy as np
from jax import lax
from jax.experimental import pallas as pl
from jax.experimental.pallas import tpu as pltpu
from jax.sharding import Mesh, PartitionSpec as P

SLOW = 128
FAST = 128
TOTAL = SLOW * FAST
HALF = SLOW // 2
ROWS = 80
FACTOR = 1.0 / (TOTAL * math.sqrt(TOTAL // 2))
NEAR = HALF // 2
RING = 4
QUARTER = HALF // RING
BLOCK = 8
LONG = 45 * 10**9


def tables():
    bf16 = jnp.bfloat16

    def angles(left, right, period):
        steps = (left[:, None] * right[None, :]) % period
        return steps.astype(np.float32) * np.float32(2.0 * math.pi / period)

    rows, first, inner = np.arange(ROWS), np.arange(HALF), np.arange(FAST)
    coarse = angles(rows, first, SLOW)
    twist = angles(rows, inner, TOTAL)
    fine = angles(inner, inner, FAST)
    cast = lambda item: item.astype(bf16)
    slow_cos, slow_sin = cast(np.cos(coarse)), cast(np.sin(coarse))
    twid_cos, twid_sin = cast(np.cos(twist)), cast(np.sin(twist))
    fast_cos, fast_sin = cast(np.cos(fine)), cast(np.sin(fine))
    weight = np.where(rows > HALF, 0.0, np.where(rows % HALF == 0, 1.0, 2.0))
    weight = weight.astype(np.float32)[:, None]
    slow_fwd = np.concatenate([slow_cos, -slow_sin], axis=0)
    slow_inv = np.concatenate(
        [cast(slow_cos.astype(np.float32) * weight), cast(-slow_sin.astype(np.float32) * weight)], axis=0
    ).T
    fast_fwd = np.block([[fast_cos, -fast_sin], [fast_sin, fast_cos]])
    fast_inv = np.block([[fast_cos, fast_sin], [-fast_sin, fast_cos]])
    twid = np.stack([twid_cos, twid_sin]).astype(np.float32)
    near = HALF // 2
    slow_half = np.stack([slow_fwd[:, :near], slow_fwd[:, near:]])
    slow_taps = np.stack([np.concatenate(
        [slow_fwd[:, (y - k) % RING * QUARTER : ((y - k) % RING + 1) * QUARTER] for k in range(RING)], axis=1
    ) for y in range(RING)])
    out_half = np.stack([slow_inv[:near], slow_inv[near:]])
    named = dict(slow_half=slow_half, slow_taps=slow_taps, out_half=out_half, out_full=slow_inv,
                 fast_fwd=fast_fwd, fast_inv=fast_inv, twid=twid)
    return {name: np.ascontiguousarray(item) for name, item in named.items()}


def dot(left, right):
    return jnp.dot(left, right, preferred_element_type=jnp.float32)


def lanes(signal):
    return jnp.concatenate([signal[j] for j in range(BLOCK)], axis=1)


def spectrum(section, twid, fast_fwd):
    wr, wi = twid[0], twid[1]
    parts = []
    for j in range(BLOCK):
        sr = section[:ROWS, j * FAST : (j + 1) * FAST]
        si = section[ROWS:, j * FAST : (j + 1) * FAST]
        parts.append(jnp.concatenate([sr * wr + si * wi, si * wr - sr * wi], axis=1).astype(jnp.bfloat16))
    return dot(jnp.concatenate(parts, axis=0), fast_fwd[...])


def inverse(product, out, slow_out, twid, fast_inv):
    section = dot(product, fast_inv[...])
    wr, wi = twid[0], twid[1]
    parts = []
    for j in range(BLOCK):
        br = section[j * ROWS : (j + 1) * ROWS, :FAST]
        bi = section[j * ROWS : (j + 1) * ROWS, FAST:]
        parts.append(jnp.concatenate([br * wr - bi * wi, bi * wr + br * wi], axis=0).astype(jnp.bfloat16))
    result = dot(slow_out, jnp.concatenate(parts, axis=1)) * FACTOR
    for j in range(BLOCK):
        out[j] = result[:, j * FAST : (j + 1) * FAST].astype(out.dtype)


def halves(spec):
    return spec[:, :FAST].astype(jnp.float32), spec[:, FAST:].astype(jnp.float32)


def joined(real, imag):
    return jnp.concatenate([real, imag], axis=1).astype(jnp.bfloat16)


def sign_of(place):
    return jnp.where(place[0] == 0, 1.0, -1.0).astype(jnp.float32)


def first_kernel(place, first, near, fast_fwd, twid, h_out):
    h_out[...] = spectrum(dot(near[0], lanes(first)), twid, fast_fwd).astype(jnp.bfloat16)


def local_kernel(place, h_in, taps, taps_table, slow_out, fast_fwd, fast_inv, twid, k_out, out):
    kr, ki = halves(spectrum(dot(taps_table[0], lanes(taps)), twid, fast_fwd).astype(jnp.bfloat16))
    ki = ki * sign_of(place)
    k_out[...] = joined(kr, ki)
    hr, hi = halves(h_in[...])
    inverse(joined(hr * kr - hi * ki, hr * ki + hi * kr), out, slow_out[0], twid, fast_inv)


def other_kernel(place, second, h_in, near, slow_out, fast_fwd, fast_inv, twid, terms):
    s_spec = spectrum(dot(near[0], lanes(second)), twid, fast_fwd).astype(jnp.bfloat16)
    (hr, hi), (sr, si) = halves(h_in[...]), halves(s_spec)
    inverse(joined(hr * sr + hi * si, (hr * si - hi * sr) * sign_of(place)), terms, slow_out[0], twid, fast_inv)


def full_spectrum(second, crossed, near, far, fast_fwd, twid):
    section = dot(near[0], lanes(second)) + dot(far[0], lanes(crossed))
    return halves(spectrum(section, twid, fast_fwd).astype(jnp.bfloat16))


def own_kernel(
    place, second, crossed, h_in, k_in, near, far, slow_out, out_full, fast_fwd, fast_inv, twid, terms, out
):
    fr, fi = full_spectrum(second, crossed, near, far, fast_fwd, twid)
    hr, hi = halves(h_in[...])
    product = joined(hr * fr + hi * fi, (hr * fi - hi * fr) * sign_of(place))
    inverse(product, terms, out_full[...], twid, fast_inv)
    kr, ki = halves(k_in[...])
    inverse(joined(kr * fr + ki * fi, kr * fi - ki * fr), out, slow_out[0], twid, fast_inv)


def cross_kernel(place, second, crossed, k_in, near, far, slow_out, fast_fwd, fast_inv, twid, out):
    fr, fi = full_spectrum(second, crossed, near, far, fast_fwd, twid)
    kr, ki = halves(k_in[...])
    inverse(joined(kr * fr + ki * fi, kr * fi - ki * fr), out, slow_out[0], twid, fast_inv)


def call(kernel, place, chans, items, outs, flops=1):
    in_specs, arrays = [], []
    for item, kind, pick in items:
        if kind == "x":
            spec = pl.BlockSpec((BLOCK,) + item.shape[1:], lambda i, p, pick=pick: (pick(p) + i, 0, 0))
        elif kind == "s":
            spec = pl.BlockSpec((BLOCK * ROWS, 2 * FAST), lambda i, p, pick=pick: (pick(p) + i, 0))
        elif kind == "t":
            spec = pl.BlockSpec((1,) + item.shape[1:], lambda i, p, pick=pick: (pick(p), 0, 0))
        else:
            spec = pl.BlockSpec(item.shape, lambda i, p, n=item.ndim: (0,) * n)
        in_specs.append(spec)
        arrays.append(item)
    out_specs, shapes = [], []
    for rows in outs:
        if rows:
            out_specs.append(pl.BlockSpec((BLOCK, rows, FAST), lambda i, p: (i, 0, 0)))
            shapes.append(jax.ShapeDtypeStruct((chans, rows, FAST), jnp.bfloat16))
        else:
            out_specs.append(pl.BlockSpec((BLOCK * ROWS, 2 * FAST), lambda i, p: (i, 0)))
            shapes.append(jax.ShapeDtypeStruct((chans * ROWS, 2 * FAST), jnp.bfloat16))
    return pl.pallas_call(
        kernel,
        grid_spec=pltpu.PrefetchScalarGridSpec(
            num_scalar_prefetch=1, grid=(chans // BLOCK,), in_specs=in_specs, out_specs=out_specs
        ),
        out_shape=shapes,
        compiler_params=pltpu.CompilerParams(vmem_limit_bytes=20 * 1024 * 1024),
        cost_estimate=pl.CostEstimate(flops=flops, bytes_accessed=1, transcendentals=0),
    )(place, *arrays)


def swap(item, axis):
    return lax.ppermute(item, axis, [(0, 1), (1, 0)])


def diagonal(item):
    return lax.ppermute(item, ("zh", "zb"), [(0, 3), (1, 2), (2, 1), (3, 0)])


def pick_half(item, index, axis=0):
    size = item.shape[axis] // 2
    return lax.dynamic_slice_in_dim(item, index * size, size, axis)


def ordered(low, near, far, axis=0):
    return jnp.concatenate([jnp.where(low, near, far), jnp.where(low, far, near)], axis=axis)


def local(values, grads, filter_taps):
    span = ("za", "x", "c")
    n_span = lax.axis_size(span)
    chans = values.shape[1] // n_span
    own = chans // 2
    consts = {name: jnp.asarray(item) for name, item in tables().items()}
    zh, zb, y = lax.axis_index("zh"), lax.axis_index("zb"), lax.axis_index("y")
    low, left = zb == 0, zh == 0
    place = jnp.stack([zb, y]).astype(jnp.int32)

    def ring(item, step):
        return lax.ppermute(item, "y", [(i, (i + step) % RING) for i in range(RING)])

    def spread(item):
        return item.reshape(2, n_span, own, FAST).transpose(1, 0, 2, 3).reshape(n_span, chans, FAST)

    def move(item):
        return lax.all_to_all(item, span, split_axis=0, concat_axis=0, tiled=True)

    taps = filter_taps.reshape(own, HALF // 8, FAST)
    across = diagonal(taps)

    v_parts, g_parts = spread(values), spread(grads)
    first_in, second_in = jnp.where(low, v_parts, g_parts), jnp.where(low, g_parts, v_parts)
    first_in, across = lax.optimization_barrier((first_in, across))
    first_raw = move(first_in)
    swapped = swap(jnp.stack([taps, across]), "zb")
    first_raw, second_in, swapped = lax.optimization_barrier((first_raw, second_in, swapped))

    first = first_raw.transpose(1, 0, 2)
    n_own = own // BLOCK
    at_start, at_own, at_far = (lambda p: 0), (lambda p: p[0] * n_own), (lambda p: (1 - p[0]) * n_own)
    here, there, row = (lambda p: p[0]), (lambda p: 1 - p[0]), (lambda p: p[1])
    near = (consts["slow_half"], "t", here)
    far = (consts["slow_half"], "t", there)
    out_near = (consts["out_half"], "t", here)
    out_start = (consts["out_half"], "t", at_start)
    out_full = (consts["out_full"], None, None)
    fast_fwd, fast_inv, twid = [(consts[name], None, None) for name in ("fast_fwd", "fast_inv", "twid")]

    (h_spec,) = call(first_kernel, place, chans, [(first, "x", at_start), near, fast_fwd, twid], [0])
    quarter = own // 2
    to_own, to_far = pick_half(first, 1 - zb), pick_half(first, zb)
    cross_own = swap(to_own, "zb")

    second = move(second_in).transpose(1, 0, 2)
    near_taps = ordered(left, taps, swapped[1], axis=1)
    far_taps = ordered(left, swapped[0], across, axis=1)
    taps = ordered(low, near_taps, far_taps)
    taps = jnp.concatenate([taps] + [ring(taps, step) for step in range(1, RING)], axis=1)
    (far_terms,) = call(
        other_kernel, place, own,
        [(second, "x", at_far), (h_spec, "s", at_far), near, out_start, fast_fwd, fast_inv, twid], [NEAR],
    )

    k_spec, local_out = call(
        local_kernel, place, chans,
        [(h_spec, "s", at_start), (taps, "x", at_start), (consts["slow_taps"], "t", row), out_near,
         fast_fwd, fast_inv, twid], [0, NEAR],
    )
    local_in, cross_own, to_far = lax.optimization_barrier((local_out.transpose(1, 0, 2), cross_own, to_far))
    local_back = move(local_in)
    cross_far = swap(to_far, "zb")
    own_terms, out_own = call(
        own_kernel, place, own,
        [(second, "x", at_own), (cross_own, "x", at_start), (h_spec, "s", at_own), (k_spec, "s", at_own),
         near, far, out_near, out_full, fast_fwd, fast_inv, twid], [HALF, NEAR],
    )

    sums = None
    for step in range(RING):
        to = (y + step) % RING
        block = jnp.stack([
            lax.dynamic_slice_in_dim(own_terms, to * QUARTER, QUARTER, 1),
            lax.dynamic_slice_in_dim(far_terms, jnp.minimum(to, 1) * QUARTER, QUARTER, 1),
        ])
        block = (ring(block, step) if step else block).astype(jnp.float32)
        sums = block if sums is None else sums + block
    (out_far,) = call(
        cross_kernel, place, own,
        [(second, "x", at_far), (cross_far, "x", at_start), (k_spec, "s", at_far), near, far, out_near,
         fast_fwd, fast_inv, twid], [NEAR], flops=LONG,
    )
    cross_in = ordered(low, out_own, out_far).transpose(1, 0, 2)
    cross_in, local_back, sums = lax.optimization_barrier((cross_in, local_back, sums))
    cross_back = move(cross_in)

    own_sum, far_sum = sums[0], jnp.where(y < RING // 2, sums[1], 0.0)
    far_here, far_there = pick_half(far_sum, zh, 1), pick_half(far_sum, 1 - zh, 1)
    own_here, own_there = pick_half(own_sum, zh, 1), pick_half(own_sum, 1 - zh, 1)
    arrived = swap(jnp.stack([far_here, own_there]).astype(jnp.bfloat16), "zb").astype(jnp.float32)
    passed = diagonal((far_there + arrived[1]).astype(jnp.bfloat16)).astype(jnp.float32)
    filter_grads = own_here + arrived[0] + passed

    def gathered(item):
        return item.reshape(n_span, 2, own, FAST).transpose(1, 0, 2, 3).reshape(values.shape)

    conv_out = gathered(jnp.where(low, local_back, cross_back))
    value_grads = gathered(jnp.where(low, cross_back, local_back))
    return conv_out, value_grads, filter_grads.reshape(filter_taps.shape)


def solution(mesh):
    fine = Mesh(mesh.devices.reshape(RING, 2, 2, 4, 4, 2), ("y", "zh", "zb", "za", "x", "c"))
    dp, ctx = ("y", "zh"), ("zb", "za", "x", "c")
    tokens = P(dp, None, ctx)
    return jax.shard_map(
        local,
        mesh=fine,
        in_specs=(tokens, tokens, P(ctx, dp)),
        out_specs=(tokens, tokens, P(ctx, dp)),
        check_vma=False,
    )
```

```python
import functools
import math

import jax
import jax.numpy as jnp
import numpy as np
from jax import lax
from jax.experimental import pallas as pl
from jax.experimental.pallas import tpu as pltpu
from jax.sharding import Mesh, PartitionSpec as P

SLOW = 128
FAST = 128
TOTAL = SLOW * FAST
HALF = SLOW // 2
ROWS = 80
FACTOR = 1.0 / (TOTAL * math.sqrt(TOTAL // 2))
NEAR = HALF // 2
RING = 4
QUARTER = HALF // RING
BLOCK = 8
LONG = 30 * 10**9


def tables():
    bf16 = jnp.bfloat16

    def angles(left, right, period):
        steps = (left[:, None] * right[None, :]) % period
        return steps.astype(np.float32) * np.float32(2.0 * math.pi / period)

    rows, first, inner = np.arange(ROWS), np.arange(HALF), np.arange(FAST)
    coarse = angles(rows, first, SLOW)
    twist = angles(rows, inner, TOTAL)
    fine = angles(inner, inner, FAST)
    cast = lambda item: item.astype(bf16)
    slow_cos, slow_sin = cast(np.cos(coarse)), cast(np.sin(coarse))
    twid_cos, twid_sin = cast(np.cos(twist)), cast(np.sin(twist))
    fast_cos, fast_sin = cast(np.cos(fine)), cast(np.sin(fine))
    weight = np.where(rows > HALF, 0.0, np.where(rows % HALF == 0, 1.0, 2.0))
    weight = weight.astype(np.float32)[:, None]
    slow_fwd = np.concatenate([slow_cos, -slow_sin], axis=0)
    slow_inv = np.concatenate(
        [cast(slow_cos.astype(np.float32) * weight), cast(-slow_sin.astype(np.float32) * weight)], axis=0
    ).T
    fast_fwd = np.block([[fast_cos, -fast_sin], [fast_sin, fast_cos]])
    fast_inv = np.block([[fast_cos, fast_sin], [-fast_sin, fast_cos]])
    twid = np.stack([twid_cos, twid_sin]).astype(np.float32)
    near = HALF // 2
    slow_half = np.stack([slow_fwd[:, :near], slow_fwd[:, near:]])
    slow_taps = np.stack([np.concatenate(
        [slow_fwd[:, (y - k) % RING * QUARTER : ((y - k) % RING + 1) * QUARTER] for k in range(RING)], axis=1
    ) for y in range(RING)])
    out_half = np.stack([slow_inv[:near], slow_inv[near:]])
    named = dict(slow_half=slow_half, slow_taps=slow_taps, out_half=out_half, out_full=slow_inv,
                 fast_fwd=fast_fwd, fast_inv=fast_inv, twid=twid)
    return {name: np.ascontiguousarray(item) for name, item in named.items()}


def dot(left, right):
    return jnp.dot(left, right, preferred_element_type=jnp.float32)


def lanes(signal):
    return jnp.concatenate([signal[j] for j in range(BLOCK)], axis=1)


def spectrum(section, twid, fast_fwd):
    wr, wi = twid[0], twid[1]
    parts = []
    for j in range(BLOCK):
        sr = section[:ROWS, j * FAST : (j + 1) * FAST]
        si = section[ROWS:, j * FAST : (j + 1) * FAST]
        parts.append(jnp.concatenate([sr * wr + si * wi, si * wr - sr * wi], axis=1).astype(jnp.bfloat16))
    return dot(jnp.concatenate(parts, axis=0), fast_fwd[...])


def inverse(product, out, slow_out, twid, fast_inv):
    section = dot(product, fast_inv[...])
    wr, wi = twid[0], twid[1]
    parts = []
    for j in range(BLOCK):
        br = section[j * ROWS : (j + 1) * ROWS, :FAST]
        bi = section[j * ROWS : (j + 1) * ROWS, FAST:]
        parts.append(jnp.concatenate([br * wr - bi * wi, bi * wr + br * wi], axis=0).astype(jnp.bfloat16))
    result = dot(slow_out, jnp.concatenate(parts, axis=1)) * FACTOR
    for j in range(BLOCK):
        out[j] = result[:, j * FAST : (j + 1) * FAST].astype(out.dtype)


def halves(spec):
    return spec[:, :FAST].astype(jnp.float32), spec[:, FAST:].astype(jnp.float32)


def joined(real, imag):
    return jnp.concatenate([real, imag], axis=1).astype(jnp.bfloat16)


def sign_of(place):
    return jnp.where(place[0] == 0, 1.0, -1.0).astype(jnp.float32)


def first_kernel(place, first, near, fast_fwd, twid, h_out):
    h_out[...] = spectrum(dot(near[0], lanes(first)), twid, fast_fwd).astype(jnp.bfloat16)


def local_kernel(place, h_in, taps, taps_table, slow_out, fast_fwd, fast_inv, twid, k_out, out):
    kr, ki = halves(spectrum(dot(taps_table[0], lanes(taps)), twid, fast_fwd).astype(jnp.bfloat16))
    ki = ki * sign_of(place)
    k_out[...] = joined(kr, ki)
    hr, hi = halves(h_in[...])
    inverse(joined(hr * kr - hi * ki, hr * ki + hi * kr), out, slow_out[0], twid, fast_inv)


def other_kernel(place, second, h_in, near, slow_out, fast_fwd, fast_inv, twid, terms):
    s_spec = spectrum(dot(near[0], lanes(second)), twid, fast_fwd).astype(jnp.bfloat16)
    (hr, hi), (sr, si) = halves(h_in[...]), halves(s_spec)
    inverse(joined(hr * sr + hi * si, (hr * si - hi * sr) * sign_of(place)), terms, slow_out[0], twid, fast_inv)


def full_spectrum(second, crossed, near, far, fast_fwd, twid):
    section = dot(near[0], lanes(second)) + dot(far[0], lanes(crossed))
    return halves(spectrum(section, twid, fast_fwd).astype(jnp.bfloat16))


def own_kernel(
    place, second, crossed, h_in, k_in, near, far, slow_out, out_full, fast_fwd, fast_inv, twid, terms, out
):
    fr, fi = full_spectrum(second, crossed, near, far, fast_fwd, twid)
    hr, hi = halves(h_in[...])
    product = joined(hr * fr + hi * fi, (hr * fi - hi * fr) * sign_of(place))
    inverse(product, terms, out_full[...], twid, fast_inv)
    kr, ki = halves(k_in[...])
    inverse(joined(kr * fr + ki * fi, kr * fi - ki * fr), out, slow_out[0], twid, fast_inv)


def cross_kernel(place, second, crossed, k_in, near, far, slow_out, fast_fwd, fast_inv, twid, out):
    fr, fi = full_spectrum(second, crossed, near, far, fast_fwd, twid)
    kr, ki = halves(k_in[...])
    inverse(joined(kr * fr + ki * fi, kr * fi - ki * fr), out, slow_out[0], twid, fast_inv)


def call(kernel, place, chans, items, outs, flops=1):
    in_specs, arrays = [], []
    for item, kind, pick in items:
        if kind == "x":
            spec = pl.BlockSpec((BLOCK,) + item.shape[1:], lambda i, p, pick=pick: (pick(p) + i, 0, 0))
        elif kind == "s":
            spec = pl.BlockSpec((BLOCK * ROWS, 2 * FAST), lambda i, p, pick=pick: (pick(p) + i, 0))
        elif kind == "t":
            spec = pl.BlockSpec((1,) + item.shape[1:], lambda i, p, pick=pick: (pick(p), 0, 0))
        else:
            spec = pl.BlockSpec(item.shape, lambda i, p, n=item.ndim: (0,) * n)
        in_specs.append(spec)
        arrays.append(item)
    out_specs, shapes = [], []
    for rows in outs:
        if rows:
            out_specs.append(pl.BlockSpec((BLOCK, rows, FAST), lambda i, p: (i, 0, 0)))
            shapes.append(jax.ShapeDtypeStruct((chans, rows, FAST), jnp.bfloat16))
        else:
            out_specs.append(pl.BlockSpec((BLOCK * ROWS, 2 * FAST), lambda i, p: (i, 0)))
            shapes.append(jax.ShapeDtypeStruct((chans * ROWS, 2 * FAST), jnp.bfloat16))
    return pl.pallas_call(
        kernel,
        grid_spec=pltpu.PrefetchScalarGridSpec(
            num_scalar_prefetch=1, grid=(chans // BLOCK,), in_specs=in_specs, out_specs=out_specs
        ),
        out_shape=shapes,
        compiler_params=pltpu.CompilerParams(vmem_limit_bytes=20 * 1024 * 1024),
        cost_estimate=pl.CostEstimate(flops=flops, bytes_accessed=1, transcendentals=0),
    )(place, *arrays)


def swap(item, axis):
    return lax.ppermute(item, axis, [(0, 1), (1, 0)])


def diagonal(item):
    return lax.ppermute(item, ("zh", "zb"), [(0, 3), (1, 2), (2, 1), (3, 0)])


def pick_half(item, index, axis=0):
    size = item.shape[axis] // 2
    return lax.dynamic_slice_in_dim(item, index * size, size, axis)


def ordered(low, near, far, axis=0):
    return jnp.concatenate([jnp.where(low, near, far), jnp.where(low, far, near)], axis=axis)


def local(values, grads, filter_taps):
    span = ("za", "x", "c")
    n_span = lax.axis_size(span)
    chans = values.shape[1] // n_span
    own = chans // 2
    consts = {name: jnp.asarray(item) for name, item in tables().items()}
    zh, zb, y = lax.axis_index("zh"), lax.axis_index("zb"), lax.axis_index("y")
    low, left = zb == 0, zh == 0
    place = jnp.stack([zb, y]).astype(jnp.int32)

    def ring(item, step):
        return lax.ppermute(item, "y", [(i, (i + step) % RING) for i in range(RING)])

    def spread(item):
        return item.reshape(2, n_span, own, FAST).transpose(1, 0, 2, 3).reshape(n_span, chans, FAST)

    def move(item):
        return lax.all_to_all(item, span, split_axis=0, concat_axis=0, tiled=True)

    taps = filter_taps.reshape(own, HALF // 8, FAST)
    across = diagonal(taps)

    v_parts, g_parts = spread(values), spread(grads)
    first_in, second_in = jnp.where(low, v_parts, g_parts), jnp.where(low, g_parts, v_parts)
    first_in, across = lax.optimization_barrier((first_in, across))
    first_raw = move(first_in)
    swapped = swap(jnp.stack([taps, across]), "zb")
    first_raw, second_in, swapped = lax.optimization_barrier((first_raw, second_in, swapped))

    first = first_raw.transpose(1, 0, 2)
    n_own = own // BLOCK
    at_start, at_own, at_far = (lambda p: 0), (lambda p: p[0] * n_own), (lambda p: (1 - p[0]) * n_own)
    here, there, row = (lambda p: p[0]), (lambda p: 1 - p[0]), (lambda p: p[1])
    near = (consts["slow_half"], "t", here)
    far = (consts["slow_half"], "t", there)
    out_near = (consts["out_half"], "t", here)
    out_start = (consts["out_half"], "t", at_start)
    out_full = (consts["out_full"], None, None)
    fast_fwd, fast_inv, twid = [(consts[name], None, None) for name in ("fast_fwd", "fast_inv", "twid")]

    (h_spec,) = call(first_kernel, place, chans, [(first, "x", at_start), near, fast_fwd, twid], [0])
    quarter = own // 2
    to_own, to_far = pick_half(first, 1 - zb), pick_half(first, zb)
    cross_own, cross_far = swap(to_own, "zb"), swap(to_far, "zb")

    second = move(second_in).transpose(1, 0, 2)
    near_taps = ordered(left, taps, swapped[1], axis=1)
    far_taps = ordered(left, swapped[0], across, axis=1)
    taps = ordered(low, near_taps, far_taps)
    taps = jnp.concatenate([taps] + [ring(taps, step) for step in range(1, RING)], axis=1)
    k_spec, local_out = call(
        local_kernel, place, chans,
        [(h_spec, "s", at_start), (taps, "x", at_start), (consts["slow_taps"], "t", row), out_near,
         fast_fwd, fast_inv, twid], [0, NEAR],
    )
    local_back = move(local_out.transpose(1, 0, 2))
    (far_terms,) = call(
        other_kernel, place, own,
        [(second, "x", at_far), (h_spec, "s", at_far), near, out_start, fast_fwd, fast_inv, twid], [NEAR],
    )

    def along(terms):
        total = None
        for step in range(RING):
            to = jnp.minimum((y + step) % RING, terms.shape[1] // QUARTER - 1)
            block = lax.dynamic_slice_in_dim(terms, to * QUARTER, QUARTER, 1)
            block = (ring(block, step) if step else block).astype(jnp.float32)
            total = block if total is None else total + block
        return total

    far_sum = jnp.where(y < RING // 2, along(far_terms), 0.0).astype(jnp.bfloat16)
    from_both = diagonal(pick_half(far_sum, 1 - zh, 1))
    cross_own, cross_far, far_sum, from_both = lax.optimization_barrier((cross_own, cross_far, far_sum, from_both))
    from_half = swap(pick_half(far_sum, zh, 1), "zb")
    own_terms, out_own = call(
        own_kernel, place, own,
        [(second, "x", at_own), (cross_own, "x", at_start), (h_spec, "s", at_own), (k_spec, "s", at_own),
         near, far, out_near, out_full, fast_fwd, fast_inv, twid], [HALF, NEAR],
    )

    own_sum = along(own_terms)
    cross_far, own_sum, from_half = lax.optimization_barrier((cross_far, own_sum, from_half))
    from_z = swap(pick_half(own_sum, 1 - zh, 1).astype(jnp.bfloat16), "zh")
    filter_grads = pick_half(own_sum, zh, 1)
    for item in (from_half, from_both, from_z):
        filter_grads = filter_grads + item.astype(jnp.float32)

    (out_far,) = call(
        cross_kernel, place, own,
        [(second, "x", at_far), (cross_far, "x", at_start), (k_spec, "s", at_far), near, far, out_near,
         fast_fwd, fast_inv, twid], [NEAR], flops=LONG,
    )
    cross_in = ordered(low, out_own, out_far).transpose(1, 0, 2)
    cross_in, local_back = lax.optimization_barrier((cross_in, local_back))
    cross_back = move(cross_in)

    def gathered(item):
        return item.reshape(n_span, 2, own, FAST).transpose(1, 0, 2, 3).reshape(values.shape)

    conv_out = gathered(jnp.where(low, local_back, cross_back))
    value_grads = gathered(jnp.where(low, cross_back, local_back))
    return conv_out, value_grads, filter_grads.reshape(filter_taps.shape)


def solution(mesh):
    fine = Mesh(mesh.devices.reshape(RING, 2, 2, 4, 4, 2), ("y", "zh", "zb", "za", "x", "c"))
    dp, ctx = ("y", "zh"), ("zb", "za", "x", "c")
    tokens = P(dp, None, ctx)
    return jax.shard_map(
        local,
        mesh=fine,
        in_specs=(tokens, tokens, P(ctx, dp)),
        out_specs=(tokens, tokens, P(ctx, dp)),
        check_vma=False,
    )
```

```python
import functools
import math

import jax
import jax.numpy as jnp
import numpy as np
from jax import lax
from jax.experimental import pallas as pl
from jax.experimental.pallas import tpu as pltpu
from jax.sharding import Mesh, PartitionSpec as P

SLOW = 128
FAST = 128
TOTAL = SLOW * FAST
HALF = SLOW // 2
ROWS = 80
FACTOR = 1.0 / (TOTAL * math.sqrt(TOTAL // 2))
BLOCK = 8


def tables():
    bf16 = jnp.bfloat16

    def angles(left, right, period):
        steps = (left[:, None] * right[None, :]) % period
        return steps.astype(np.float32) * np.float32(2.0 * math.pi / period)

    rows, first, inner = np.arange(ROWS), np.arange(HALF), np.arange(FAST)
    coarse = angles(rows, first, SLOW)
    twist = angles(rows, inner, TOTAL)
    fine = angles(inner, inner, FAST)
    cast = lambda item: item.astype(bf16)
    slow_cos, slow_sin = cast(np.cos(coarse)), cast(np.sin(coarse))
    twid_cos, twid_sin = cast(np.cos(twist)), cast(np.sin(twist))
    fast_cos, fast_sin = cast(np.cos(fine)), cast(np.sin(fine))
    weight = np.where(rows > HALF, 0.0, np.where(rows % HALF == 0, 1.0, 2.0))
    weight = weight.astype(np.float32)[:, None]
    slow_fwd = np.concatenate([slow_cos, -slow_sin], axis=0)
    slow_inv = np.concatenate(
        [cast(slow_cos.astype(np.float32) * weight), cast(-slow_sin.astype(np.float32) * weight)], axis=0
    ).T
    fast_fwd = np.block([[fast_cos, -fast_sin], [fast_sin, fast_cos]])
    fast_inv = np.block([[fast_cos, fast_sin], [-fast_sin, fast_cos]])
    twid = np.stack([twid_cos, twid_sin]).astype(np.float32)
    return tuple(map(np.ascontiguousarray, (slow_fwd, slow_inv, fast_fwd, fast_inv, twid)))


def turned(places):
    blocks = np.split(tables()[0], places, axis=1)
    return np.stack([np.concatenate([blocks[(y - k) % places] for k in range(places)], axis=1) for y in range(places)])


def dot(left, right):
    return jnp.dot(left, right, preferred_element_type=jnp.float32)


def forward(signal, slow_fwd, twid, fast_fwd):
    lanes = jnp.concatenate([signal[j] for j in range(BLOCK)], axis=1)
    section = dot(slow_fwd[...], lanes)
    wr, wi = twid[0], twid[1]
    parts = []
    for j in range(BLOCK):
        sr = section[:ROWS, j * FAST : (j + 1) * FAST]
        si = section[ROWS:, j * FAST : (j + 1) * FAST]
        parts.append(jnp.concatenate([sr * wr + si * wi, si * wr - sr * wi], axis=1).astype(jnp.bfloat16))
    return dot(jnp.concatenate(parts, axis=0), fast_fwd[...]).astype(jnp.bfloat16)


def inverse(spectrum, out, slow_inv, twid, fast_inv):
    section = dot(spectrum, fast_inv[...])
    wr, wi = twid[0], twid[1]
    parts = []
    for j in range(BLOCK):
        br = section[j * ROWS : (j + 1) * ROWS, :FAST]
        bi = section[j * ROWS : (j + 1) * ROWS, FAST:]
        parts.append(jnp.concatenate([br * wr - bi * wi, bi * wr + br * wi], axis=0).astype(jnp.bfloat16))
    result = dot(slow_inv[...], jnp.concatenate(parts, axis=1)) * FACTOR
    for j in range(BLOCK):
        out[j] = result[:, j * FAST : (j + 1) * FAST].astype(out.dtype)


def halves(spectrum):
    return spectrum[:, :FAST].astype(jnp.float32), spectrum[:, FAST:].astype(jnp.float32)


def joined(real, imag):
    return jnp.concatenate([real, imag], axis=1).astype(jnp.bfloat16)


def spectra_kernel(taps, slow_fwd, slow_inv, fast_fwd, fast_inv, twid, k_out):
    k_out[...] = forward(taps, slow_fwd, twid, fast_fwd)


def conv_kernel(values, k_in, slow_fwd, slow_inv, fast_fwd, fast_inv, twid, u_out, conv):
    u_spec = forward(values, slow_fwd, twid, fast_fwd)
    u_out[...] = u_spec
    (ur, ui), (kr, ki) = halves(u_spec), halves(k_in[...])
    inverse(joined(ur * kr - ui * ki, ur * ki + ui * kr), conv, slow_inv, twid, fast_inv)


def taps_kernel(grads, u_in, slow_fwd, slow_inv, fast_fwd, fast_inv, twid, z_out, taps):
    z_spec = forward(grads, slow_fwd, twid, fast_fwd)
    z_out[...] = z_spec
    (ur, ui), (zr, zi) = halves(u_in[...]), halves(z_spec)
    inverse(joined(ur * zr + ui * zi, ur * zi - ui * zr), taps, slow_inv, twid, fast_inv)


def back_kernel(z_in, k_in, slow_fwd, slow_inv, fast_fwd, fast_inv, twid, back):
    (zr, zi), (kr, ki) = halves(z_in[...]), halves(k_in[...])
    inverse(joined(kr * zr + ki * zi, kr * zi - ki * zr), back, slow_inv, twid, fast_inv)


def call(kernel, signals, outs, consts, start=0):
    item, kind = signals[-1]
    chans = item.shape[0] // ROWS if kind == "s" else item.shape[0]
    specs = {
        "y": pl.BlockSpec((BLOCK, HALF, FAST), lambda i: (start // BLOCK + i, 0, 0)),
        "x": pl.BlockSpec((BLOCK, HALF, FAST), lambda i: (i, 0, 0)),
        "s": pl.BlockSpec((BLOCK * ROWS, 2 * FAST), lambda i: (i, 0)),
    }
    shapes = {
        "x": jax.ShapeDtypeStruct((chans, HALF, FAST), jnp.bfloat16),
        "s": jax.ShapeDtypeStruct((chans * ROWS, 2 * FAST), jnp.bfloat16),
    }
    whole = [pl.BlockSpec(item.shape, functools.partial(lambda n, i: (0,) * n, item.ndim)) for item in consts]
    return pl.pallas_call(
        kernel,
        grid=(chans // BLOCK,),
        in_specs=[specs[kind] for _, kind in signals] + whole,
        out_specs=[specs[kind] for kind in outs],
        out_shape=[shapes[kind] for kind in outs],
        compiler_params=pltpu.CompilerParams(vmem_limit_bytes=20 * 1024 * 1024),
        cost_estimate=pl.CostEstimate(flops=1, bytes_accessed=1, transcendentals=0),
    )(*[item for item, _ in signals], *consts)


def exchange(item, axis):
    return lax.ppermute(item, axis, [(0, 1), (1, 0)])


def local(values, grads, filter_taps):
    ctx = ("zl", "x", "c")
    groups = lax.axis_size(ctx)
    chans = values.shape[1] // groups
    consts = tuple(jnp.asarray(item) for item in tables())
    high = lax.axis_index("zh")
    row = lax.axis_index("y")
    n_row = lax.axis_size("y")
    wide = filter_taps.shape[1]

    def move(item):
        return lax.all_to_all(item, ctx, split_axis=0, concat_axis=0, tiled=True)

    def outward(item):
        return move(item.transpose(1, 0, 2)).reshape(1, groups * chans, FAST)

    def ring(item, step):
        return lax.ppermute(item, "y", [(i, (i + step) % n_row) for i in range(n_row)])

    blocks = filter_taps.reshape(chans, wide // FAST, FAST)
    other = exchange(blocks, "zh")
    pair = jnp.concatenate([jnp.where(high == 0, blocks, other), jnp.where(high == 0, other, blocks)], axis=1)
    taps = jnp.concatenate([pair] + [ring(pair, step) for step in range(1, n_row)], axis=1)
    slow_taps = lax.dynamic_index_in_dim(jnp.asarray(turned(n_row)), row, 0, keepdims=False)
    (k_spec,) = call(spectra_kernel, [(taps, "x")], "s", (slow_taps,) + consts[1:])

    both = jnp.concatenate([values.reshape(groups, chans, FAST), grads.reshape(groups, chans, FAST)], axis=1)
    mine, k_spec = lax.optimization_barrier((move(both), k_spec))
    mine = mine.transpose(1, 0, 2)
    u_spec, conv = call(conv_kernel, [(mine, "x"), (k_spec, "s")], "sx", consts)
    conv_out = outward(conv)
    z_spec, terms = call(taps_kernel, [(mine, "y"), (u_spec, "s")], "sx", consts, chans)
    (back,) = call(back_kernel, [(z_spec, "s"), (k_spec, "s")], "x", consts)

    depth = HALF // n_row
    total = None
    for step in range(n_row):
        block = lax.dynamic_slice_in_dim(terms, (row + step) % n_row * depth, depth, 1)
        block = (ring(block, step) if step else block).astype(jnp.float32)
        total = block if total is None else total + block
    back, total = lax.optimization_barrier((back, total))
    value_grads = outward(back)
    kept = lax.dynamic_slice_in_dim(total, high * (depth // 2), depth // 2, 1)
    sent = lax.dynamic_slice_in_dim(total, (1 - high) * (depth // 2), depth // 2, 1).astype(jnp.bfloat16)
    filter_grads = (kept + exchange(sent, "zh").astype(jnp.float32)).reshape(filter_taps.shape)
    return conv_out, value_grads, filter_grads


def solution(mesh):
    fine = Mesh(mesh.devices.reshape(4, 2, 8, 4, 2), ("y", "zh", "zl", "x", "c"))
    dp, ctx = ("y", "zh"), ("zl", "x", "c")
    tokens = P(dp, None, ctx)
    return jax.shard_map(
        local,
        mesh=fine,
        in_specs=(tokens, tokens, P(ctx, dp)),
        out_specs=(tokens, tokens, P(ctx, dp)),
        check_vma=False,
    )
```

```python
import functools
import math

import jax
import jax.numpy as jnp
import numpy as np
from jax import lax
from jax.experimental import pallas as pl
from jax.experimental.pallas import tpu as pltpu
from jax.sharding import Mesh, PartitionSpec as P

SLOW = 128
FAST = 128
TOTAL = SLOW * FAST
HALF = SLOW // 2
ROWS = 80
FACTOR = 1.0 / (TOTAL * math.sqrt(TOTAL // 2))
BLOCK = 8


def tables():
    bf16 = jnp.bfloat16

    def angles(left, right, period):
        steps = (left[:, None] * right[None, :]) % period
        return steps.astype(np.float32) * np.float32(2.0 * math.pi / period)

    rows, first, inner = np.arange(ROWS), np.arange(HALF), np.arange(FAST)
    coarse = angles(rows, first, SLOW)
    twist = angles(rows, inner, TOTAL)
    fine = angles(inner, inner, FAST)
    cast = lambda item: item.astype(bf16)
    slow_cos, slow_sin = cast(np.cos(coarse)), cast(np.sin(coarse))
    twid_cos, twid_sin = cast(np.cos(twist)), cast(np.sin(twist))
    fast_cos, fast_sin = cast(np.cos(fine)), cast(np.sin(fine))
    weight = np.where(rows > HALF, 0.0, np.where(rows % HALF == 0, 1.0, 2.0))
    weight = weight.astype(np.float32)[:, None]
    slow_fwd = np.concatenate([slow_cos, -slow_sin], axis=0)
    slow_inv = np.concatenate(
        [cast(slow_cos.astype(np.float32) * weight), cast(-slow_sin.astype(np.float32) * weight)], axis=0
    ).T
    fast_fwd = np.block([[fast_cos, -fast_sin], [fast_sin, fast_cos]])
    fast_inv = np.block([[fast_cos, fast_sin], [-fast_sin, fast_cos]])
    twid = np.stack([twid_cos, twid_sin]).astype(np.float32)
    return tuple(map(np.ascontiguousarray, (slow_fwd, slow_inv, fast_fwd, fast_inv, twid)))


def turned(places):
    blocks = np.split(tables()[0], places, axis=1)
    return np.stack([np.concatenate([blocks[(y - k) % places] for k in range(places)], axis=1) for y in range(places)])


def dot(left, right):
    return jnp.dot(left, right, preferred_element_type=jnp.float32)


def forward(signal, slow_fwd, twid, fast_fwd):
    lanes = jnp.concatenate([signal[j] for j in range(BLOCK)], axis=1)
    section = dot(slow_fwd[...], lanes)
    wr, wi = twid[0], twid[1]
    parts = []
    for j in range(BLOCK):
        sr = section[:ROWS, j * FAST : (j + 1) * FAST]
        si = section[ROWS:, j * FAST : (j + 1) * FAST]
        parts.append(jnp.concatenate([sr * wr + si * wi, si * wr - sr * wi], axis=1).astype(jnp.bfloat16))
    return dot(jnp.concatenate(parts, axis=0), fast_fwd[...]).astype(jnp.bfloat16)


def inverse(spectrum, out, slow_inv, twid, fast_inv):
    section = dot(spectrum, fast_inv[...])
    wr, wi = twid[0], twid[1]
    parts = []
    for j in range(BLOCK):
        br = section[j * ROWS : (j + 1) * ROWS, :FAST]
        bi = section[j * ROWS : (j + 1) * ROWS, FAST:]
        parts.append(jnp.concatenate([br * wr - bi * wi, bi * wr + br * wi], axis=0).astype(jnp.bfloat16))
    result = dot(slow_inv[...], jnp.concatenate(parts, axis=1)) * FACTOR
    for j in range(BLOCK):
        out[j] = result[:, j * FAST : (j + 1) * FAST].astype(out.dtype)


def halves(spectrum):
    return spectrum[:, :FAST].astype(jnp.float32), spectrum[:, FAST:].astype(jnp.float32)


def joined(real, imag):
    return jnp.concatenate([real, imag], axis=1).astype(jnp.bfloat16)


def spectra_kernel(taps, slow_fwd, slow_inv, fast_fwd, fast_inv, twid, k_out):
    k_out[...] = forward(taps, slow_fwd, twid, fast_fwd)


def products_kernel(
    values, grads, k_in, slow_fwd, slow_inv, fast_fwd, fast_inv, twid, taps, outs
):
    ur, ui = halves(forward(values, slow_fwd, twid, fast_fwd))
    zr, zi = halves(forward(grads, slow_fwd, twid, fast_fwd))
    inverse(joined(ur * zr + ui * zi, ur * zi - ui * zr), taps, slow_inv, twid, fast_inv)
    kr, ki = halves(k_in[...])
    inverse(joined(ur * kr - ui * ki, ur * ki + ui * kr), outs.at[0], slow_inv, twid, fast_inv)
    inverse(joined(kr * zr + ki * zi, kr * zi - ki * zr), outs.at[1], slow_inv, twid, fast_inv)


def call(kernel, signals, outs, consts, start=0):
    item, kind = signals[-1]
    chans = item.shape[0] // ROWS if kind == "s" else item.shape[0]
    specs = {
        "w": pl.BlockSpec((2, BLOCK, HALF, FAST), lambda i: (0, i, 0, 0)),
        "y": pl.BlockSpec((BLOCK, HALF, FAST), lambda i: (start // BLOCK + i, 0, 0)),
        "x": pl.BlockSpec((BLOCK, HALF, FAST), lambda i: (i, 0, 0)),
        "s": pl.BlockSpec((BLOCK * ROWS, 2 * FAST), lambda i: (i, 0)),
    }
    shapes = {
        "w": jax.ShapeDtypeStruct((2, chans, HALF, FAST), jnp.bfloat16),
        "x": jax.ShapeDtypeStruct((chans, HALF, FAST), jnp.bfloat16),
        "s": jax.ShapeDtypeStruct((chans * ROWS, 2 * FAST), jnp.bfloat16),
    }
    whole = [pl.BlockSpec(item.shape, functools.partial(lambda n, i: (0,) * n, item.ndim)) for item in consts]
    return pl.pallas_call(
        kernel,
        grid=(chans // BLOCK,),
        in_specs=[specs[kind] for _, kind in signals] + whole,
        out_specs=[specs[kind] for kind in outs],
        out_shape=[shapes[kind] for kind in outs],
        compiler_params=pltpu.CompilerParams(vmem_limit_bytes=20 * 1024 * 1024),
        cost_estimate=pl.CostEstimate(flops=1, bytes_accessed=1, transcendentals=0),
    )(*[item for item, _ in signals], *consts)


def exchange(item, axis):
    return lax.ppermute(item, axis, [(0, 1), (1, 0)])


def local(values, grads, filter_taps):
    ctx = ("zl", "x", "c")
    groups = lax.axis_size(ctx)
    chans = values.shape[1] // groups
    consts = tuple(jnp.asarray(item) for item in tables())
    high = lax.axis_index("zh")
    row = lax.axis_index("y")
    n_row = lax.axis_size("y")
    wide = filter_taps.shape[1]

    def move(item):
        return lax.all_to_all(item, ctx, split_axis=0, concat_axis=0, tiled=True)

    def ring(item, step):
        return lax.ppermute(item, "y", [(i, (i + step) % n_row) for i in range(n_row)])

    blocks = filter_taps.reshape(chans, wide // FAST, FAST)
    other = exchange(blocks, "zh")
    pair = jnp.concatenate([jnp.where(high == 0, blocks, other), jnp.where(high == 0, other, blocks)], axis=1)
    taps = jnp.concatenate([pair] + [ring(pair, step) for step in range(1, n_row)], axis=1)
    slow_taps = lax.dynamic_index_in_dim(jnp.asarray(turned(n_row)), row, 0, keepdims=False)
    (k_spec,) = call(spectra_kernel, [(taps, "x")], "s", (slow_taps,) + consts[1:])

    both = jnp.concatenate([values.reshape(groups, chans, FAST), grads.reshape(groups, chans, FAST)], axis=1)
    mine, k_spec = lax.optimization_barrier((move(both), k_spec))
    mine = mine.transpose(1, 0, 2)
    terms, outs = call(products_kernel, [(mine, "x"), (mine, "y"), (k_spec, "s")], "xw", consts, chans)
    arrived = move(outs.reshape(2 * chans, HALF, FAST).transpose(1, 0, 2))
    conv_out = arrived[:, :chans].reshape(values.shape)
    value_grads = arrived[:, chans:].reshape(values.shape)

    depth = HALF // n_row
    total = None
    for step in range(n_row):
        block = lax.dynamic_slice_in_dim(terms, (row + step) % n_row * depth, depth, 1)
        block = (ring(block, step) if step else block).astype(jnp.float32)
        total = block if total is None else total + block
    kept = lax.dynamic_slice_in_dim(total, high * (depth // 2), depth // 2, 1)
    sent = lax.dynamic_slice_in_dim(total, (1 - high) * (depth // 2), depth // 2, 1).astype(jnp.bfloat16)
    filter_grads = (kept + exchange(sent, "zh").astype(jnp.float32)).reshape(filter_taps.shape)
    return conv_out, value_grads, filter_grads


def solution(mesh):
    fine = Mesh(mesh.devices.reshape(4, 2, 8, 4, 2), ("y", "zh", "zl", "x", "c"))
    dp, ctx = ("y", "zh"), ("zl", "x", "c")
    tokens = P(dp, None, ctx)
    return jax.shard_map(
        local,
        mesh=fine,
        in_specs=(tokens, tokens, P(ctx, dp)),
        out_specs=(tokens, tokens, P(ctx, dp)),
        check_vma=False,
    )
```

```python
import functools
import math

import jax
import jax.numpy as jnp
import numpy as np
from jax import lax
from jax.experimental import pallas as pl
from jax.experimental.pallas import tpu as pltpu
from jax.sharding import Mesh, PartitionSpec as P

SLOW = 128
FAST = 128
TOTAL = SLOW * FAST
HALF = SLOW // 2
ROWS = 80
FACTOR = 1.0 / (TOTAL * math.sqrt(TOTAL // 2))
BLOCK = 8
BESIDE = 80 * 10**9


def tables():
    bf16 = jnp.bfloat16

    def angles(left, right, period):
        steps = (left[:, None] * right[None, :]) % period
        return steps.astype(np.float32) * np.float32(2.0 * math.pi / period)

    rows, first, inner = np.arange(ROWS), np.arange(HALF), np.arange(FAST)
    coarse = angles(rows, first, SLOW)
    twist = angles(rows, inner, TOTAL)
    fine = angles(inner, inner, FAST)
    cast = lambda item: item.astype(bf16)
    slow_cos, slow_sin = cast(np.cos(coarse)), cast(np.sin(coarse))
    twid_cos, twid_sin = cast(np.cos(twist)), cast(np.sin(twist))
    fast_cos, fast_sin = cast(np.cos(fine)), cast(np.sin(fine))
    weight = np.where(rows > HALF, 0.0, np.where(rows % HALF == 0, 1.0, 2.0))
    weight = weight.astype(np.float32)[:, None]
    slow_fwd = np.concatenate([slow_cos, -slow_sin], axis=0)
    slow_inv = np.concatenate(
        [cast(slow_cos.astype(np.float32) * weight), cast(-slow_sin.astype(np.float32) * weight)], axis=0
    ).T
    fast_fwd = np.block([[fast_cos, -fast_sin], [fast_sin, fast_cos]])
    fast_inv = np.block([[fast_cos, fast_sin], [-fast_sin, fast_cos]])
    twid = np.stack([twid_cos, twid_sin]).astype(np.float32)
    return tuple(map(np.ascontiguousarray, (slow_fwd, slow_inv, fast_fwd, fast_inv, twid)))


def turned(places):
    blocks = np.split(tables()[0], places, axis=1)
    return np.stack([np.concatenate([blocks[(y - k) % places] for k in range(places)], axis=1) for y in range(places)])


def dot(left, right):
    return jnp.dot(left, right, preferred_element_type=jnp.float32)


def forward(signal, slow_fwd, twid, fast_fwd):
    lanes = jnp.concatenate([signal[j] for j in range(BLOCK)], axis=1)
    section = dot(slow_fwd[...], lanes)
    wr, wi = twid[0], twid[1]
    parts = []
    for j in range(BLOCK):
        sr = section[:ROWS, j * FAST : (j + 1) * FAST]
        si = section[ROWS:, j * FAST : (j + 1) * FAST]
        parts.append(jnp.concatenate([sr * wr + si * wi, si * wr - sr * wi], axis=1).astype(jnp.bfloat16))
    return dot(jnp.concatenate(parts, axis=0), fast_fwd[...]).astype(jnp.bfloat16)


def inverse(spectrum, out, slow_inv, twid, fast_inv):
    section = dot(spectrum, fast_inv[...])
    wr, wi = twid[0], twid[1]
    parts = []
    for j in range(BLOCK):
        br = section[j * ROWS : (j + 1) * ROWS, :FAST]
        bi = section[j * ROWS : (j + 1) * ROWS, FAST:]
        parts.append(jnp.concatenate([br * wr - bi * wi, bi * wr + br * wi], axis=0).astype(jnp.bfloat16))
    result = dot(slow_inv[...], jnp.concatenate(parts, axis=1)) * FACTOR
    for j in range(BLOCK):
        out[j] = result[:, j * FAST : (j + 1) * FAST].astype(out.dtype)


def halves(spectrum):
    return spectrum[:, :FAST].astype(jnp.float32), spectrum[:, FAST:].astype(jnp.float32)


def joined(real, imag):
    return jnp.concatenate([real, imag], axis=1).astype(jnp.bfloat16)


def spectra_kernel(taps, slow_fwd, slow_inv, fast_fwd, fast_inv, twid, k_out):
    k_out[...] = forward(taps, slow_fwd, twid, fast_fwd)


def products_kernel(
    values, grads, k_in, slow_fwd, slow_inv, fast_fwd, fast_inv, twid, taps, outs
):
    ur, ui = halves(forward(values, slow_fwd, twid, fast_fwd))
    zr, zi = halves(forward(grads, slow_fwd, twid, fast_fwd))
    inverse(joined(ur * zr + ui * zi, ur * zi - ui * zr), taps, slow_inv, twid, fast_inv)
    kr, ki = halves(k_in[...])
    inverse(joined(ur * kr - ui * ki, ur * ki + ui * kr), outs.at[0], slow_inv, twid, fast_inv)
    inverse(joined(kr * zr + ki * zi, kr * zi - ki * zr), outs.at[1], slow_inv, twid, fast_inv)


def call(kernel, signals, outs, consts, start=0, flops=1):
    item, kind = signals[-1]
    chans = item.shape[0] // ROWS if kind == "s" else item.shape[0]
    specs = {
        "w": pl.BlockSpec((2, BLOCK, HALF, FAST), lambda i: (0, i, 0, 0)),
        "y": pl.BlockSpec((BLOCK, HALF, FAST), lambda i: (start // BLOCK + i, 0, 0)),
        "x": pl.BlockSpec((BLOCK, HALF, FAST), lambda i: (i, 0, 0)),
        "s": pl.BlockSpec((BLOCK * ROWS, 2 * FAST), lambda i: (i, 0)),
    }
    shapes = {
        "w": jax.ShapeDtypeStruct((2, chans, HALF, FAST), jnp.bfloat16),
        "x": jax.ShapeDtypeStruct((chans, HALF, FAST), jnp.bfloat16),
        "s": jax.ShapeDtypeStruct((chans * ROWS, 2 * FAST), jnp.bfloat16),
    }
    whole = [pl.BlockSpec(item.shape, functools.partial(lambda n, i: (0,) * n, item.ndim)) for item in consts]
    return pl.pallas_call(
        kernel,
        grid=(chans // BLOCK,),
        in_specs=[specs[kind] for _, kind in signals] + whole,
        out_specs=[specs[kind] for kind in outs],
        out_shape=[shapes[kind] for kind in outs],
        compiler_params=pltpu.CompilerParams(vmem_limit_bytes=20 * 1024 * 1024),
        cost_estimate=pl.CostEstimate(flops=flops, bytes_accessed=1, transcendentals=0),
    )(*[item for item, _ in signals], *consts)


def exchange(item, axis):
    return lax.ppermute(item, axis, [(0, 1), (1, 0)])


def local(values, grads, filter_taps):
    ctx = ("zl", "x", "c")
    groups = lax.axis_size(ctx)
    chans = values.shape[1] // groups
    consts = tuple(jnp.asarray(item) for item in tables())
    high = lax.axis_index("zh")
    row = lax.axis_index("y")
    n_row = lax.axis_size("y")
    wide = filter_taps.shape[1]

    def move(item):
        return lax.all_to_all(item, ctx, split_axis=0, concat_axis=0, tiled=True)

    def ring(item, step):
        return lax.ppermute(item, "y", [(i, (i + step) % n_row) for i in range(n_row)])

    blocks = filter_taps.reshape(chans, wide // FAST, FAST)
    other = exchange(blocks, "zh")
    pair = jnp.concatenate([jnp.where(high == 0, blocks, other), jnp.where(high == 0, other, blocks)], axis=1)
    taps = jnp.concatenate([pair] + [ring(pair, step) for step in range(1, n_row)], axis=1)
    slow_taps = lax.dynamic_index_in_dim(jnp.asarray(turned(n_row)), row, 0, keepdims=False)
    (k_spec,) = call(spectra_kernel, [(taps, "x")], "s", (slow_taps,) + consts[1:], flops=BESIDE)

    both = jnp.concatenate([values.reshape(groups, chans, FAST), grads.reshape(groups, chans, FAST)], axis=1)
    mine, k_spec = lax.optimization_barrier((move(both), k_spec))
    mine = mine.transpose(1, 0, 2)
    terms, outs = call(products_kernel, [(mine, "x"), (mine, "y"), (k_spec, "s")], "xw", consts, chans)
    arrived = move(outs.reshape(2 * chans, HALF, FAST).transpose(1, 0, 2))
    conv_out = arrived[:, :chans].reshape(values.shape)
    value_grads = arrived[:, chans:].reshape(values.shape)

    depth = HALF // n_row
    total = None
    for step in range(n_row):
        block = lax.dynamic_slice_in_dim(terms, (row + step) % n_row * depth, depth, 1)
        block = (ring(block, step) if step else block).astype(jnp.float32)
        total = block if total is None else total + block
    kept = lax.dynamic_slice_in_dim(total, high * (depth // 2), depth // 2, 1)
    sent = lax.dynamic_slice_in_dim(total, (1 - high) * (depth // 2), depth // 2, 1).astype(jnp.bfloat16)
    filter_grads = (kept + exchange(sent, "zh").astype(jnp.float32)).reshape(filter_taps.shape)
    return conv_out, value_grads, filter_grads


def solution(mesh):
    fine = Mesh(mesh.devices.reshape(4, 2, 8, 4, 2), ("y", "zh", "zl", "x", "c"))
    dp, ctx = ("y", "zh"), ("zl", "x", "c")
    tokens = P(dp, None, ctx)
    return jax.shard_map(
        local,
        mesh=fine,
        in_specs=(tokens, tokens, P(ctx, dp)),
        out_specs=(tokens, tokens, P(ctx, dp)),
        check_vma=False,
    )
```

```python
import functools
import math

import jax
import jax.numpy as jnp
import numpy as np
from jax import lax
from jax.experimental import pallas as pl
from jax.experimental.pallas import tpu as pltpu
from jax.sharding import Mesh, PartitionSpec as P

SLOW = 128
FAST = 128
TOTAL = SLOW * FAST
HALF = SLOW // 2
ROWS = 80
FACTOR = 1.0 / (TOTAL * math.sqrt(TOTAL // 2))
BLOCK = 16
BESIDE = 80 * 10**9


def tables():
    bf16 = jnp.bfloat16

    def angles(left, right, period):
        steps = (left[:, None] * right[None, :]) % period
        return steps.astype(np.float32) * np.float32(2.0 * math.pi / period)

    rows, first, inner = np.arange(ROWS), np.arange(HALF), np.arange(FAST)
    coarse = angles(rows, first, SLOW)
    twist = angles(rows, inner, TOTAL)
    fine = angles(inner, inner, FAST)
    cast = lambda item: item.astype(bf16)
    slow_cos, slow_sin = cast(np.cos(coarse)), cast(np.sin(coarse))
    twid_cos, twid_sin = cast(np.cos(twist)), cast(np.sin(twist))
    fast_cos, fast_sin = cast(np.cos(fine)), cast(np.sin(fine))
    weight = np.where(rows > HALF, 0.0, np.where(rows % HALF == 0, 1.0, 2.0))
    weight = weight.astype(np.float32)[:, None]
    slow_fwd = np.concatenate([slow_cos, -slow_sin], axis=0)
    slow_inv = np.concatenate(
        [cast(slow_cos.astype(np.float32) * weight), cast(-slow_sin.astype(np.float32) * weight)], axis=0
    ).T
    fast_fwd = np.block([[fast_cos, -fast_sin], [fast_sin, fast_cos]])
    fast_inv = np.block([[fast_cos, fast_sin], [-fast_sin, fast_cos]])
    twid = np.stack([twid_cos, twid_sin]).astype(np.float32)
    return tuple(map(np.ascontiguousarray, (slow_fwd, slow_inv, fast_fwd, fast_inv, twid)))


def turned(places):
    blocks = np.split(tables()[0], places, axis=1)
    return np.stack([np.concatenate([blocks[(y - k) % places] for k in range(places)], axis=1) for y in range(places)])


def dot(left, right):
    return jnp.dot(left, right, preferred_element_type=jnp.float32)


def forward(signal, slow_fwd, twid, fast_fwd):
    lanes = jnp.concatenate([signal[j] for j in range(BLOCK)], axis=1)
    section = dot(slow_fwd[...], lanes)
    wr, wi = twid[0], twid[1]
    parts = []
    for j in range(BLOCK):
        sr = section[:ROWS, j * FAST : (j + 1) * FAST]
        si = section[ROWS:, j * FAST : (j + 1) * FAST]
        parts.append(jnp.concatenate([sr * wr + si * wi, si * wr - sr * wi], axis=1).astype(jnp.bfloat16))
    return dot(jnp.concatenate(parts, axis=0), fast_fwd[...]).astype(jnp.bfloat16)


def inverse(spectrum, slow_inv, twid, fast_inv):
    section = dot(spectrum, fast_inv[...])
    wr, wi = twid[0], twid[1]
    parts = []
    for j in range(BLOCK):
        br = section[j * ROWS : (j + 1) * ROWS, :FAST]
        bi = section[j * ROWS : (j + 1) * ROWS, FAST:]
        parts.append(jnp.concatenate([br * wr - bi * wi, bi * wr + br * wi], axis=0).astype(jnp.bfloat16))
    result = dot(slow_inv[...], jnp.concatenate(parts, axis=1)) * FACTOR
    return jnp.stack([result[:, j * FAST : (j + 1) * FAST].astype(jnp.bfloat16) for j in range(BLOCK)])


def halves(spectrum):
    return spectrum[:, :FAST].astype(jnp.float32), spectrum[:, FAST:].astype(jnp.float32)


def joined(real, imag):
    return jnp.concatenate([real, imag], axis=1).astype(jnp.bfloat16)


def spectra_kernel(taps, slow_fwd, slow_inv, fast_fwd, fast_inv, twid, k_out):
    k_out[...] = forward(taps, slow_fwd, twid, fast_fwd)


def products_kernel(values, grads, k_in, slow_fwd, slow_inv, fast_fwd, fast_inv, twid, terms, outs):
    ur, ui = halves(forward(jnp.swapaxes(values[...], 0, 1), slow_fwd, twid, fast_fwd))
    zr, zi = halves(forward(jnp.swapaxes(grads[...], 0, 1), slow_fwd, twid, fast_fwd))
    terms[...] = inverse(joined(ur * zr + ui * zi, ur * zi - ui * zr), slow_inv, twid, fast_inv)
    kr, ki = halves(k_in[...])
    conv = inverse(joined(ur * kr - ui * ki, ur * ki + ui * kr), slow_inv, twid, fast_inv)
    outs[:, 0] = jnp.swapaxes(conv, 0, 1)
    back = inverse(joined(kr * zr + ki * zi, kr * zi - ki * zr), slow_inv, twid, fast_inv)
    outs[:, 1] = jnp.swapaxes(back, 0, 1)


def call(kernel, chans, items, outs, consts, flops=1):
    whole = [pl.BlockSpec(item.shape, functools.partial(lambda n, i: (0,) * n, item.ndim)) for item in consts]
    return pl.pallas_call(
        kernel,
        grid=(chans // BLOCK,),
        in_specs=[pl.BlockSpec(block, index) for _, block, index in items] + whole,
        out_specs=[pl.BlockSpec(block, index) for _, block, index in outs],
        out_shape=[jax.ShapeDtypeStruct(shape, jnp.bfloat16) for shape, _, _ in outs],
        compiler_params=pltpu.CompilerParams(vmem_limit_bytes=30 * 1024 * 1024),
        cost_estimate=pl.CostEstimate(flops=flops, bytes_accessed=1, transcendentals=0),
    )(*[item for item, _, _ in items], *consts)


def exchange(item, axis):
    return lax.ppermute(item, axis, [(0, 1), (1, 0)])


def local(values, grads, filter_taps):
    ctx = ("zl", "x", "c")
    groups = lax.axis_size(ctx)
    chans = values.shape[1] // groups
    consts = tuple(jnp.asarray(item) for item in tables())
    high = lax.axis_index("zh")
    row = lax.axis_index("y")
    n_row = lax.axis_size("y")
    wide = filter_taps.shape[1]

    def move(item):
        return lax.all_to_all(item, ctx, split_axis=0, concat_axis=0, tiled=True)

    def ring(item, step):
        return lax.ppermute(item, "y", [(i, (i + step) % n_row) for i in range(n_row)])

    both = jnp.concatenate([values.reshape(groups, chans, FAST), grads.reshape(groups, chans, FAST)], axis=1)
    both, filter_taps = lax.optimization_barrier((both, filter_taps))

    blocks = filter_taps.reshape(chans, wide // FAST, FAST)
    other = exchange(blocks, "zh")
    pair = jnp.concatenate([jnp.where(high == 0, blocks, other), jnp.where(high == 0, other, blocks)], axis=1)
    taps = jnp.concatenate([pair] + [ring(pair, step) for step in range(1, n_row)], axis=1)
    slow_taps = lax.dynamic_index_in_dim(jnp.asarray(turned(n_row)), row, 0, keepdims=False)
    rows = ((chans * ROWS, 2 * FAST), (BLOCK * ROWS, 2 * FAST), lambda i: (i, 0))
    lines = ((chans, HALF, FAST), (BLOCK, HALF, FAST), lambda i: (i, 0, 0))
    (k_spec,) = call(
        spectra_kernel, chans, [(taps,) + lines[1:]], [rows], (slow_taps,) + consts[1:], flops=BESIDE
    )

    mine, k_spec = lax.optimization_barrier((move(both), k_spec))
    across = (HALF, BLOCK, FAST)
    terms, outs = call(
        products_kernel, chans,
        [(mine, across, lambda i: (0, i, 0)), (mine, across, lambda i: (0, chans // BLOCK + i, 0)),
         (k_spec,) + rows[1:]],
        [lines, ((HALF, 2, chans, FAST), (HALF, 2, BLOCK, FAST), lambda i: (0, 0, i, 0))], consts,
    )
    arrived = move(outs.reshape(groups, 2 * chans, FAST))
    conv_out = arrived[:, :chans].reshape(values.shape)
    value_grads = arrived[:, chans:].reshape(values.shape)

    depth = HALF // n_row
    total = None
    for step in range(n_row):
        block = lax.dynamic_slice_in_dim(terms, (row + step) % n_row * depth, depth, 1)
        block = (ring(block, step) if step else block).astype(jnp.float32)
        total = block if total is None else total + block
    kept = lax.dynamic_slice_in_dim(total, high * (depth // 2), depth // 2, 1)
    sent = lax.dynamic_slice_in_dim(total, (1 - high) * (depth // 2), depth // 2, 1).astype(jnp.bfloat16)
    filter_grads = (kept + exchange(sent, "zh").astype(jnp.float32)).reshape(filter_taps.shape)
    return conv_out, value_grads, filter_grads


def solution(mesh):
    fine = Mesh(mesh.devices.reshape(4, 2, 8, 4, 2), ("y", "zh", "zl", "x", "c"))
    dp, ctx = ("y", "zh"), ("zl", "x", "c")
    tokens = P(dp, None, ctx)
    return jax.shard_map(
        local,
        mesh=fine,
        in_specs=(tokens, tokens, P(ctx, dp)),
        out_specs=(tokens, tokens, P(ctx, dp)),
        check_vma=False,
    )
```

```python
import functools
import math

import jax
import jax.numpy as jnp
import numpy as np
from jax import lax
from jax.experimental import pallas as pl
from jax.experimental.pallas import tpu as pltpu
from jax.sharding import Mesh, PartitionSpec as P

SLOW = 128
FAST = 128
TOTAL = SLOW * FAST
HALF = SLOW // 2
ROWS = 72
FACTOR = 1.0 / (TOTAL * math.sqrt(TOTAL // 2))
BLOCK = 16
BESIDE = 80 * 10**9


def tables():
    bf16 = jnp.bfloat16

    def angles(left, right, period):
        steps = (left[:, None] * right[None, :]) % period
        return steps.astype(np.float32) * np.float32(2.0 * math.pi / period)

    rows, first, inner = np.arange(ROWS), np.arange(HALF), np.arange(FAST)
    coarse = angles(rows, first, SLOW)
    twist = angles(rows, inner, TOTAL)
    fine = angles(inner, inner, FAST)
    cast = lambda item: item.astype(bf16)
    slow_cos, slow_sin = cast(np.cos(coarse)), cast(np.sin(coarse))
    twid_cos, twid_sin = cast(np.cos(twist)), cast(np.sin(twist))
    fast_cos, fast_sin = cast(np.cos(fine)), cast(np.sin(fine))
    weight = np.where(rows > HALF, 0.0, np.where(rows % HALF == 0, 1.0, 2.0))
    weight = weight.astype(np.float32)[:, None]
    slow_fwd = np.concatenate([slow_cos, -slow_sin], axis=0)
    slow_inv = np.concatenate(
        [cast(slow_cos.astype(np.float32) * weight), cast(-slow_sin.astype(np.float32) * weight)], axis=0
    ).T
    fast_fwd = np.block([[fast_cos, -fast_sin], [fast_sin, fast_cos]])
    fast_inv = np.block([[fast_cos, fast_sin], [-fast_sin, fast_cos]])
    twid = np.stack([twid_cos, twid_sin]).astype(np.float32)
    return tuple(map(np.ascontiguousarray, (slow_fwd, slow_inv, fast_fwd, fast_inv, twid)))


def turned(places):
    blocks = np.split(tables()[0], places, axis=1)
    return np.stack([np.concatenate([blocks[(y - k) % places] for k in range(places)], axis=1) for y in range(places)])


def dot(left, right):
    return jnp.dot(left, right, preferred_element_type=jnp.float32)


def forward(signal, slow_fwd, twid, fast_fwd):
    lanes = jnp.concatenate([signal[j] for j in range(BLOCK)], axis=1)
    section = dot(slow_fwd[...], lanes)
    wr, wi = twid[0], twid[1]
    parts = []
    for j in range(BLOCK):
        sr = section[:ROWS, j * FAST : (j + 1) * FAST]
        si = section[ROWS:, j * FAST : (j + 1) * FAST]
        parts.append(jnp.concatenate([sr * wr + si * wi, si * wr - sr * wi], axis=1))
    return dot(jnp.concatenate(parts, axis=0).astype(jnp.bfloat16), fast_fwd[...]).astype(jnp.bfloat16)


def inverse(spectrum, slow_inv, twid, fast_inv):
    section = dot(spectrum, fast_inv[...])
    wr, wi = twid[0], twid[1]
    parts = []
    for j in range(BLOCK):
        br = section[j * ROWS : (j + 1) * ROWS, :FAST]
        bi = section[j * ROWS : (j + 1) * ROWS, FAST:]
        parts.append(jnp.concatenate([br * wr - bi * wi, bi * wr + br * wi], axis=0).astype(jnp.bfloat16))
    result = dot(slow_inv[...], jnp.concatenate(parts, axis=1)) * FACTOR
    return jnp.stack([result[:, j * FAST : (j + 1) * FAST].astype(jnp.bfloat16) for j in range(BLOCK)])


def halves(spectrum):
    return spectrum[:, :FAST].astype(jnp.float32), spectrum[:, FAST:].astype(jnp.float32)


def joined(real, imag):
    return jnp.concatenate([real, imag], axis=1).astype(jnp.bfloat16)


def spectra_kernel(taps, slow_fwd, slow_inv, fast_fwd, fast_inv, twid, k_out):
    k_out[...] = forward(taps, slow_fwd, twid, fast_fwd)


def outs_kernel(values, grads, k_in, slow_fwd, slow_inv, fast_fwd, fast_inv, twid, outs):
    ur, ui = halves(forward(jnp.swapaxes(values[...], 0, 1), slow_fwd, twid, fast_fwd))
    kr, ki = halves(k_in[...])
    conv = inverse(joined(ur * kr - ui * ki, ur * ki + ui * kr), slow_inv, twid, fast_inv)
    outs[:, 0] = jnp.swapaxes(conv, 0, 1)
    zr, zi = halves(forward(jnp.swapaxes(grads[...], 0, 1), slow_fwd, twid, fast_fwd))
    back = inverse(joined(kr * zr + ki * zi, kr * zi - ki * zr), slow_inv, twid, fast_inv)
    outs[:, 1] = jnp.swapaxes(back, 0, 1)


def terms_kernel(values, grads, slow_fwd, slow_inv, fast_fwd, fast_inv, twid, terms):
    ur, ui = halves(forward(jnp.swapaxes(values[...], 0, 1), slow_fwd, twid, fast_fwd))
    zr, zi = halves(forward(jnp.swapaxes(grads[...], 0, 1), slow_fwd, twid, fast_fwd))
    terms[...] = inverse(joined(ur * zr + ui * zi, ur * zi - ui * zr), slow_inv, twid, fast_inv)


def call(kernel, chans, items, outs, consts, flops=1):
    whole = [pl.BlockSpec(item.shape, functools.partial(lambda n, i: (0,) * n, item.ndim)) for item in consts]
    return pl.pallas_call(
        kernel,
        grid=(chans // BLOCK,),
        in_specs=[pl.BlockSpec(block, index) for _, block, index in items] + whole,
        out_specs=[pl.BlockSpec(block, index) for _, block, index in outs],
        out_shape=[jax.ShapeDtypeStruct(shape, jnp.bfloat16) for shape, _, _ in outs],
        compiler_params=pltpu.CompilerParams(vmem_limit_bytes=30 * 1024 * 1024),
        cost_estimate=pl.CostEstimate(flops=flops, bytes_accessed=1, transcendentals=0),
    )(*[item for item, _, _ in items], *consts)


def exchange(item, axis):
    return lax.ppermute(item, axis, [(0, 1), (1, 0)])


def local(values, grads, filter_taps):
    ctx = ("zl", "x", "c")
    groups = lax.axis_size(ctx)
    chans = values.shape[1] // groups
    consts = tuple(jnp.asarray(item) for item in tables())
    high = lax.axis_index("zh")
    row = lax.axis_index("y")
    n_row = lax.axis_size("y")
    wide = filter_taps.shape[1]

    def move(item):
        return lax.all_to_all(item, ctx, split_axis=0, concat_axis=0, tiled=True)

    def ring(item, step):
        return lax.ppermute(item, "y", [(i, (i + step) % n_row) for i in range(n_row)])

    both = jnp.concatenate([values.reshape(groups, chans, FAST), grads.reshape(groups, chans, FAST)], axis=1)
    both, filter_taps = lax.optimization_barrier((both, filter_taps))

    blocks = filter_taps.reshape(chans, wide // FAST, FAST)
    other = exchange(blocks, "zh")
    pair = jnp.concatenate([jnp.where(high == 0, blocks, other), jnp.where(high == 0, other, blocks)], axis=1)
    taps = jnp.concatenate([pair] + [ring(pair, step) for step in range(1, n_row)], axis=1)
    slow_taps = lax.dynamic_index_in_dim(jnp.asarray(turned(n_row)), row, 0, keepdims=False)
    rows = ((chans * ROWS, 2 * FAST), (BLOCK * ROWS, 2 * FAST), lambda i: (i, 0))
    lines = ((chans, HALF, FAST), (BLOCK, HALF, FAST), lambda i: (i, 0, 0))
    (k_spec,) = call(
        spectra_kernel, chans, [(taps,) + lines[1:]], [rows], (slow_taps,) + consts[1:], flops=BESIDE
    )

    mine, k_spec = lax.optimization_barrier((move(both), k_spec))
    across = (HALF, BLOCK, FAST)
    signals = [(mine, across, lambda i: (0, i, 0)), (mine, across, lambda i: (0, chans // BLOCK + i, 0))]
    (outs,) = call(
        outs_kernel, chans, signals + [(k_spec,) + rows[1:]],
        [((HALF, 2, chans, FAST), (HALF, 2, BLOCK, FAST), lambda i: (0, 0, i, 0))], consts,
    )
    (terms,) = call(terms_kernel, chans, signals, [lines], consts)
    arrived = move(outs.reshape(groups, 2 * chans, FAST))
    conv_out = arrived[:, :chans].reshape(values.shape)
    value_grads = arrived[:, chans:].reshape(values.shape)

    depth = HALF // n_row
    total = None
    for step in range(n_row):
        block = lax.dynamic_slice_in_dim(terms, (row + step) % n_row * depth, depth, 1)
        block = (ring(block, step) if step else block).astype(jnp.float32)
        total = block if total is None else total + block
    kept = lax.dynamic_slice_in_dim(total, high * (depth // 2), depth // 2, 1)
    sent = lax.dynamic_slice_in_dim(total, (1 - high) * (depth // 2), depth // 2, 1).astype(jnp.bfloat16)
    filter_grads = (kept + exchange(sent, "zh").astype(jnp.float32)).reshape(filter_taps.shape)
    return conv_out, value_grads, filter_grads


def solution(mesh):
    fine = Mesh(mesh.devices.reshape(4, 2, 8, 4, 2), ("y", "zh", "zl", "x", "c"))
    dp, ctx = ("y", "zh"), ("zl", "x", "c")
    tokens = P(dp, None, ctx)
    return jax.shard_map(
        local,
        mesh=fine,
        in_specs=(tokens, tokens, P(ctx, dp)),
        out_specs=(tokens, tokens, P(ctx, dp)),
        check_vma=False,
    )
```

```python
import functools
import math

import jax
import jax.numpy as jnp
import numpy as np
from jax import lax
from jax.experimental import pallas as pl
from jax.experimental.pallas import tpu as pltpu
from jax.sharding import Mesh, PartitionSpec as P

SLOW = 128
FAST = 128
TOTAL = SLOW * FAST
HALF = SLOW // 2
ROWS = 72
FACTOR = 1.0 / (TOTAL * math.sqrt(TOTAL // 2))
BLOCK = 32
BESIDE = 80 * 10**9


def tables():
    bf16 = jnp.bfloat16

    def angles(left, right, period):
        steps = (left[:, None] * right[None, :]) % period
        return steps.astype(np.float32) * np.float32(2.0 * math.pi / period)

    rows, first, inner = np.arange(ROWS), np.arange(HALF), np.arange(FAST)
    coarse = angles(rows, first, SLOW)
    twist = angles(rows, inner, TOTAL)
    fine = angles(inner, inner, FAST)
    cast = lambda item: item.astype(bf16)
    slow_cos, slow_sin = cast(np.cos(coarse)), cast(np.sin(coarse))
    twid_cos, twid_sin = cast(np.cos(twist)), cast(np.sin(twist))
    fast_cos, fast_sin = cast(np.cos(fine)), cast(np.sin(fine))
    weight = np.where(rows > HALF, 0.0, np.where(rows % HALF == 0, 1.0, 2.0))
    weight = weight.astype(np.float32)[:, None]
    slow_fwd = np.concatenate([slow_cos, -slow_sin], axis=0)
    slow_inv = np.concatenate(
        [cast(slow_cos.astype(np.float32) * weight), cast(-slow_sin.astype(np.float32) * weight)], axis=0
    ).T
    fast_fwd = np.block([[fast_cos, -fast_sin], [fast_sin, fast_cos]])
    fast_inv = np.block([[fast_cos, fast_sin], [-fast_sin, fast_cos]])
    twid = np.stack([twid_cos, twid_sin]).astype(np.float32)
    return tuple(map(np.ascontiguousarray, (slow_fwd, slow_inv, fast_fwd, fast_inv, twid)))


def turned(places):
    blocks = np.split(tables()[0], places, axis=1)
    return np.stack([np.concatenate([blocks[(y - k) % places] for k in range(places)], axis=1) for y in range(places)])


def dot(left, right):
    return jnp.dot(left, right, preferred_element_type=jnp.float32)


def forward(signal, slow_fwd, twid, fast_fwd):
    lanes = jnp.concatenate([signal[j] for j in range(BLOCK)], axis=1)
    section = dot(slow_fwd[...], lanes)
    wr, wi = twid[0], twid[1]
    parts = []
    for j in range(BLOCK):
        sr = section[:ROWS, j * FAST : (j + 1) * FAST]
        si = section[ROWS:, j * FAST : (j + 1) * FAST]
        parts.append(jnp.concatenate([sr * wr + si * wi, si * wr - sr * wi], axis=1))
    return dot(jnp.concatenate(parts, axis=0).astype(jnp.bfloat16), fast_fwd[...]).astype(jnp.bfloat16)


def inverse(spectrum, slow_inv, twid, fast_inv):
    section = dot(spectrum, fast_inv[...])
    wr, wi = twid[0], twid[1]
    parts = []
    for j in range(BLOCK):
        br = section[j * ROWS : (j + 1) * ROWS, :FAST]
        bi = section[j * ROWS : (j + 1) * ROWS, FAST:]
        parts.append(jnp.concatenate([br * wr - bi * wi, bi * wr + br * wi], axis=0).astype(jnp.bfloat16))
    result = dot(slow_inv[...], jnp.concatenate(parts, axis=1)) * FACTOR
    return jnp.stack([result[:, j * FAST : (j + 1) * FAST].astype(jnp.bfloat16) for j in range(BLOCK)])


def halves(spectrum):
    return spectrum[:, :FAST].astype(jnp.float32), spectrum[:, FAST:].astype(jnp.float32)


def joined(real, imag):
    return jnp.concatenate([real, imag], axis=1).astype(jnp.bfloat16)


def spectra_kernel(taps, slow_fwd, slow_inv, fast_fwd, fast_inv, twid, k_out):
    k_out[...] = forward(taps, slow_fwd, twid, fast_fwd)


def outs_kernel(values, grads, k_in, slow_fwd, slow_inv, fast_fwd, fast_inv, twid, outs):
    ur, ui = halves(forward(jnp.swapaxes(values[...], 0, 1), slow_fwd, twid, fast_fwd))
    kr, ki = halves(k_in[...])
    conv = inverse(joined(ur * kr - ui * ki, ur * ki + ui * kr), slow_inv, twid, fast_inv)
    outs[:, 0] = jnp.swapaxes(conv, 0, 1)
    zr, zi = halves(forward(jnp.swapaxes(grads[...], 0, 1), slow_fwd, twid, fast_fwd))
    back = inverse(joined(kr * zr + ki * zi, kr * zi - ki * zr), slow_inv, twid, fast_inv)
    outs[:, 1] = jnp.swapaxes(back, 0, 1)


def terms_kernel(values, grads, slow_fwd, slow_inv, fast_fwd, fast_inv, twid, terms):
    ur, ui = halves(forward(jnp.swapaxes(values[...], 0, 1), slow_fwd, twid, fast_fwd))
    zr, zi = halves(forward(jnp.swapaxes(grads[...], 0, 1), slow_fwd, twid, fast_fwd))
    terms[...] = inverse(joined(ur * zr + ui * zi, ur * zi - ui * zr), slow_inv, twid, fast_inv)


def call(kernel, chans, items, outs, consts, flops=1):
    whole = [pl.BlockSpec(item.shape, functools.partial(lambda n, i: (0,) * n, item.ndim)) for item in consts]
    return pl.pallas_call(
        kernel,
        grid=(chans // BLOCK,),
        in_specs=[pl.BlockSpec(block, index) for _, block, index in items] + whole,
        out_specs=[pl.BlockSpec(block, index) for _, block, index in outs],
        out_shape=[jax.ShapeDtypeStruct(shape, jnp.bfloat16) for shape, _, _ in outs],
        compiler_params=pltpu.CompilerParams(vmem_limit_bytes=30 * 1024 * 1024),
        cost_estimate=pl.CostEstimate(flops=flops, bytes_accessed=1, transcendentals=0),
    )(*[item for item, _, _ in items], *consts)


def exchange(item, axis):
    return lax.ppermute(item, axis, [(0, 1), (1, 0)])


def local(values, grads, filter_taps):
    ctx = ("zl", "x", "c")
    groups = lax.axis_size(ctx)
    chans = values.shape[1] // groups
    consts = tuple(jnp.asarray(item) for item in tables())
    high = lax.axis_index("zh")
    row = lax.axis_index("y")
    n_row = lax.axis_size("y")
    wide = filter_taps.shape[1]

    def move(item):
        return lax.all_to_all(item, ctx, split_axis=0, concat_axis=0, tiled=True)

    def ring(item, step):
        return lax.ppermute(item, "y", [(i, (i + step) % n_row) for i in range(n_row)])

    both = jnp.concatenate([values.reshape(groups, chans, FAST), grads.reshape(groups, chans, FAST)], axis=1)
    both, filter_taps = lax.optimization_barrier((both, filter_taps))

    blocks = filter_taps.reshape(chans, wide // FAST, FAST)
    other = exchange(blocks, "zh")
    pair = jnp.concatenate([jnp.where(high == 0, blocks, other), jnp.where(high == 0, other, blocks)], axis=1)
    taps = jnp.concatenate([pair] + [ring(pair, step) for step in range(1, n_row)], axis=1)
    slow_taps = lax.dynamic_index_in_dim(jnp.asarray(turned(n_row)), row, 0, keepdims=False)
    rows = ((chans * ROWS, 2 * FAST), (BLOCK * ROWS, 2 * FAST), lambda i: (i, 0))
    lines = ((chans, HALF, FAST), (BLOCK, HALF, FAST), lambda i: (i, 0, 0))
    (k_spec,) = call(
        spectra_kernel, chans, [(taps,) + lines[1:]], [rows], (slow_taps,) + consts[1:], flops=BESIDE
    )

    mine, k_spec = lax.optimization_barrier((move(both), k_spec))
    across = (HALF, BLOCK, FAST)
    signals = [(mine, across, lambda i: (0, i, 0)), (mine, across, lambda i: (0, chans // BLOCK + i, 0))]
    (outs,) = call(
        outs_kernel, chans, signals + [(k_spec,) + rows[1:]],
        [((HALF, 2, chans, FAST), (HALF, 2, BLOCK, FAST), lambda i: (0, 0, i, 0))], consts,
    )
    (terms,) = call(terms_kernel, chans, signals, [lines], consts)
    arrived = move(outs.reshape(groups, 2 * chans, FAST))
    conv_out = arrived[:, :chans].reshape(values.shape)
    value_grads = arrived[:, chans:].reshape(values.shape)

    depth = HALF // n_row
    total = None
    for step in range(n_row):
        block = lax.dynamic_slice_in_dim(terms, (row + step) % n_row * depth, depth, 1)
        block = (ring(block, step) if step else block).astype(jnp.float32)
        total = block if total is None else total + block
    kept = lax.dynamic_slice_in_dim(total, high * (depth // 2), depth // 2, 1)
    sent = lax.dynamic_slice_in_dim(total, (1 - high) * (depth // 2), depth // 2, 1).astype(jnp.bfloat16)
    filter_grads = (kept + exchange(sent, "zh").astype(jnp.float32)).reshape(filter_taps.shape)
    return conv_out, value_grads, filter_grads


def solution(mesh):
    fine = Mesh(mesh.devices.reshape(4, 2, 8, 4, 2), ("y", "zh", "zl", "x", "c"))
    dp, ctx = ("y", "zh"), ("zl", "x", "c")
    tokens = P(dp, None, ctx)
    return jax.shard_map(
        local,
        mesh=fine,
        in_specs=(tokens, tokens, P(ctx, dp)),
        out_specs=(tokens, tokens, P(ctx, dp)),
        check_vma=False,
    )
```
